256 devices in a mesh: facet: 32 (over y_lo, z, core), half: 4 (over x), sub: 2 (over y_hi).
Axes of the slice: x: 4, y: 4 (y_hi: 2, y_lo: 2; y = y_hi * 2 + y_lo), z: 8, core: 2. Of those that a mesh axis runs over, the one named last changes fastest.
Arguments:
- facets: bfloat16 [32, 2, 2048, 2048], P('facet', None, ('half', 'sub')), may hold values from -6 to 6
- weights: float32 [512, 16, 512], P('facet', ('half', 'sub')), may hold values from 0.25 to 4
- facet_offsets: int32 [32, 2], replicated, may hold values from 0 to 511
- subgrid_offsets: int32 [16], replicated, may hold values from 0 to 2047
- column: int32 [1], replicated, may hold values from 0 to 2047
Outputs:
- facet_update: bfloat16 [32, 2, 2048, 2048], P('facet', None, ('half', 'sub'))
- spectra: float32 [512, 16, 2, 512], P('facet', ('half', 'sub'))
The draws below stay inside these ranges and needn't reach their ends.
All inputs are finite; a program needn't handle non-finite values.
Results may differ from the reference program's by a relative error of at most 0.025.
Values may be sent and summed in bfloat16 or wider, within the bound.
A program may use at most 128 MiB of HBM per device.

```python
import math
import jax
import jax.numpy as jnp
from jax import lax

YF = 2048
M = 128
XM = 512
SUBS = 16
FACETS = 32


def plant(drawn, stream_key, least, high):
    extent = drawn.shape
    spot = [jax.random.randint(jax.random.fold_in(stream_key, axis), (), 0, extent[axis]) for axis in range(len(extent))]
    drawn = drawn.at[tuple(spot)].set(least)
    longest = extent.index(max(extent))
    spot[longest] = (spot[longest] + 1) % extent[longest]
    return drawn.at[tuple(spot)].set(high)


def block_levels(key, dims, cuts, smallest, high):
    loudness, own = 1.0, jax.random.fold_in(key, 6)
    for position, parts in cuts:
        heights = jnp.exp(jax.random.uniform(jax.random.fold_in(own, position), (parts,), jnp.float32, smallest / len(cuts), high / len(cuts)))
        loudness = loudness * jnp.repeat(heights, dims[position] // parts).reshape([-1 if axis == position else 1 for axis in range(len(dims))])
    return loudness


def bell_draw(key, extent, scale, most, shards=(), held_as=jnp.bfloat16):
    result = scale * jax.random.normal(key, extent, jnp.float32)
    if shards:
        result = result * block_levels(key, extent, shards, -0.22, 0.18)
    return jnp.clip(result, -most, most).astype(held_as)


def setup_inputs(seed: int = 0) -> dict:
    key_list = jax.random.split(jax.random.key(seed), 6)
    return {
        "facets": bell_draw(key_list[0], (FACETS, 2, YF, YF), 1.0, 6.0, ((0, 32), (2, 8))),
        "weights": jnp.clip(jnp.exp(math.log(4.0) - 2.7725887 * jax.random.uniform(key_list[1], (XM, SUBS, XM), jnp.float32) ** block_levels(key_list[1], (XM, SUBS, XM), ((0, 32), (1, 8)), -0.2, 0.2)), 0.25, 4.0),
        "facet_offsets": plant(jax.random.randint(key_list[2], (FACETS, 2), 0, XM), jax.random.fold_in(key_list[2], 1), 0, XM - 1).astype(jnp.int32),
        "subgrid_offsets": plant(jax.random.randint(key_list[3], (SUBS,), 0, YF), jax.random.fold_in(key_list[3], 1), 0, YF - 1).astype(jnp.int32),
        "column": jax.random.randint(key_list[4], (1,), 0, YF).astype(jnp.int32),
    }


HI = lax.Precision.HIGHEST

def wave(freq, pos, n):
    turns = freq[:, None] * pos[None, :] % n
    angle = turns.astype(jnp.float32) * (2.0 * math.pi / n)
    return (jnp.cos(angle), jnp.sin(angle))

def facet_table(freq, pos, n):
    cosine, sine = wave(freq, pos, n)
    shaped = (jnp.sin(math.pi * (pos.astype(jnp.float32) + 0.5) / n) ** 2)[None, :] / math.sqrt(n)
    return ((cosine * shaped).astype(jnp.bfloat16), (-sine * shaped).astype(jnp.bfloat16))

def cmat(form, l_real, l_imag, r_real, r_imag):
    real = jnp.einsum(form, l_real, r_real, precision=HI) - jnp.einsum(form, l_imag, r_imag, precision=HI)
    imag = jnp.einsum(form, l_real, r_imag, precision=HI) + jnp.einsum(form, l_imag, r_real, precision=HI)
    return (real, imag)

def reference(facets, weights, facet_offsets, subgrid_offsets, column):
    near = jnp.arange(M, dtype=jnp.int32)
    span = jnp.arange(XM, dtype=jnp.int32)
    every = jnp.arange(YF, dtype=jnp.int32)
    column_freq = (column[0] + near) % YF
    q_real, q_imag = facet_table(column_freq, every, YF)
    sub_freq = ((subgrid_offsets[:, None] + near[None, :]) % YF).reshape(-1)
    p_real, p_imag = facet_table(sub_freq, every, YF)
    scale = 1.0 / math.sqrt(XM)
    cos_f, sin_f = wave(span, span, XM)
    f_real = cos_f * scale
    f_imag = -sin_f * scale

    def place(offset):
        rows = (span[:, None] == ((offset[0] + near) % XM)[None, :]).astype(jnp.float32)
        cols = (span[:, None] == ((offset[1] + near) % XM)[None, :]).astype(jnp.float32)
        return (rows, cols)

    def forward(carry, item):
        planes, offset = item
        f32 = jnp.float32
        a_real = (jnp.dot(planes[0], q_real.T, preferred_element_type=f32) - jnp.dot(planes[1], q_imag.T, preferred_element_type=f32)).astype(jnp.bfloat16)
        a_imag = (jnp.dot(planes[0], q_imag.T, preferred_element_type=f32) + jnp.dot(planes[1], q_real.T, preferred_element_type=f32)).astype(jnp.bfloat16)
        c_real = (jnp.dot(p_real, a_real, preferred_element_type=f32) - jnp.dot(p_imag, a_imag, preferred_element_type=f32)).reshape(SUBS, M, M)
        c_imag = (jnp.dot(p_real, a_imag, preferred_element_type=f32) + jnp.dot(p_imag, a_real, preferred_element_type=f32)).reshape(SUBS, M, M)
        rows, cols = place(offset)
        g_real = carry[0] + jnp.einsum('aj,sjk,bk->sab', rows, c_real, cols, precision=HI)
        g_imag = carry[1] + jnp.einsum('aj,sjk,bk->sab', rows, c_imag, cols, precision=HI)
        return ((g_real, g_imag), None)
    start = (jnp.zeros((SUBS, XM, XM), jnp.float32), jnp.zeros((SUBS, XM, XM), jnp.float32))
    (g_real, g_imag), _ = lax.scan(forward, start, (facets, facet_offsets))
    t_real, t_imag = cmat('ab,sbc->sac', f_real, f_imag, g_real, g_imag)
    hat_real, hat_imag = cmat('sac,cd->sad', t_real, t_imag, f_real, f_imag)
    resident = jnp.transpose(weights, (1, 0, 2))
    h_real = resident * hat_real
    h_imag = resident * hat_imag
    spectra = jnp.transpose(jnp.stack([h_real, h_imag], 1), (2, 0, 1, 3))
    u_real, u_imag = cmat('ab,sbc->sac', f_real, -f_imag, h_real, h_imag)
    space_real, space_imag = cmat('sac,cd->sad', u_real, u_imag, f_real, -f_imag)
    gain = 2.0 * math.sqrt(YF / M)

    def backward(offset):
        f32 = jnp.float32
        rows, cols = place(offset)
        d_real = jnp.einsum('aj,sab,bk->sjk', rows, space_real, cols, precision=HI).astype(jnp.bfloat16).reshape(SUBS * M, M)
        d_imag = jnp.einsum('aj,sab,bk->sjk', rows, space_imag, cols, precision=HI).astype(jnp.bfloat16).reshape(SUBS * M, M)
        e_real = (jnp.dot(p_real.T, d_real, preferred_element_type=f32) + jnp.dot(p_imag.T, d_imag, preferred_element_type=f32)).astype(jnp.bfloat16)
        e_imag = (jnp.dot(p_real.T, d_imag, preferred_element_type=f32) - jnp.dot(p_imag.T, d_real, preferred_element_type=f32)).astype(jnp.bfloat16)
        w_real = jnp.dot(e_real, q_real, preferred_element_type=f32) + jnp.dot(e_imag, q_imag, preferred_element_type=f32)
        w_imag = jnp.dot(e_imag, q_real, preferred_element_type=f32) - jnp.dot(e_real, q_imag, preferred_element_type=f32)
        return (jnp.stack([w_real, w_imag]) * gain).astype(jnp.bfloat16)
    update = lax.map(backward, facet_offsets)
    return (update, spectra)
```

```python
import functools
import math

import jax
import jax.numpy as jnp
from jax import lax
from jax.experimental import pallas as pl
from jax.experimental.pallas import tpu as pltpu
from jax.sharding import PartitionSpec as P

YF = 2048
M = 128
XM = 512
SUBS = 16
FACETS = 32
TEAM = 8
PAIR = 2
ROWS = 256
BLOCK = 16
MESH = pl.DeviceIdType.MESH
F32 = jnp.float32
BF16 = jnp.bfloat16


def cis(turn, n):
    quarter = n // 4
    q = lax.shift_right_logical(turn + n // 8, quarter.bit_length() - 1)
    x = (turn - q * quarter).astype(F32) * (2.0 * math.pi / n)
    z = x * x
    s = x + x * z * (-1.6666654611e-1 + z * (8.3321608736e-3 - 1.9515295891e-4 * z))
    c = 1.0 - 0.5 * z + z * z * (4.166664568298827e-2 + z * (-1.388731625493765e-3 + 2.443315711809948e-5 * z))
    swap = (q & 1) == 1
    cosine = jnp.where(swap, s, c)
    sine = jnp.where(swap, c, s)
    cosine = jnp.where(((q + 1) & 2) != 0, -cosine, cosine)
    sine = jnp.where((q & 2) != 0, -sine, sine)
    return cosine, sine


def iota(shape, dim):
    return lax.broadcasted_iota(jnp.int32, shape, dim)


def taper(pos):
    _, s = cis(2 * pos + 1, 4 * YF)
    return s * s * (1.0 / math.sqrt(YF))


def dot(a, b):
    return jnp.dot(a, b, preferred_element_type=F32)


def dot_t(a, b):
    return lax.dot_general(a, b, (((0,), (0,)), ((), ())), preferred_element_type=F32)


def round_trip(
    facets, weights, foff, soff, col,
    et_out, q_out, spectra,
    x_buf, hi_c, hi_s, lo_c, lo_s, p_tab, f_tab, r_tab, perm,
    send1, recv1, send2, recv2, send3, recv3, send4, recv4,
    x_sem, s1, r1, s2, r2, s3, r3, s4, r4,
):
    mine = lax.axis_index("facet")
    half = lax.axis_index("half")
    sub = lax.axis_index("sub")
    member = half * 2 + sub

    def mate(i):
        t = lax.rem(member + i, TEAM)
        return t, {"half": t // 2, "sub": lax.rem(t, 2)}

    def peer(i):
        t = lax.rem(mine + i, FACETS)
        return t, {"facet": t}

    load = pltpu.make_async_copy(facets, x_buf, x_sem)
    load.start()

    barrier = pltpu.get_barrier_semaphore()

    @pl.loop(1, TEAM)
    def _(i):
        pl.semaphore_signal(barrier, inc=1, device_id=mate(i)[1], device_id_type=MESH)

    @pl.loop(1, FACETS)
    def _(i):
        pl.semaphore_signal(barrier, inc=1, device_id=peer(i)[1], device_id_type=MESH)

    y = iota((8, YF), 1)
    c, s = cis(((col[0] + 16 * iota((8, YF), 0)) & (YF - 1)) * y & (YF - 1), YF)
    hi_c[...] = c
    hi_s[...] = s
    c, s = cis(iota((16, YF), 0) * iota((16, YF), 1) & (YF - 1), YF)
    w = taper(iota((1, YF), 1))
    lo_c[...] = c * w
    lo_s[...] = s * w

    @pl.loop(0, 8)
    def _(a):
        hc, hs = hi_c[pl.ds(a, 1), :], hi_s[pl.ds(a, 1), :]
        lc, ls = lo_c[...], lo_s[...]
        at = pl.multiple_of(a * 16, 16)
        q_out[pl.ds(at, 16), :] = (hc * lc - hs * ls).astype(BF16)
        q_out[pl.ds(at + M, 16), :] = (-(hs * lc + hc * ls)).astype(BF16)

    turn = foff[mine, 1] & (M - 1)
    k, c = iota((2 * M, 2 * M), 0), iota((2 * M, 2 * M), 1)
    same = ((k & (M - 1)) == ((c - turn) & (M - 1))) & ((k < M) == (c < M))
    perm[...] = jnp.where(same, 1.0, 0.0).astype(BF16)

    first = member * ROWS
    pos = first + iota((16, ROWS), 1)
    c, s = cis(iota((16, ROWS), 0) * pos & (YF - 1), YF)
    w = taper(first + iota((1, ROWS), 1))
    lc, ls = c * w, s * w

    @pl.loop(0, SUBS)
    def _(u):
        freq = (soff[u] + 16 * iota((8, ROWS), 0)) & (YF - 1)
        hc, hs = cis(freq * (first + iota((8, ROWS), 1)) & (YF - 1), YF)
        for a in range(8):
            c, s = hc[a : a + 1], hs[a : a + 1]
            p_tab[u, 16 * a : 16 * a + 16, :] = (c * lc - s * ls).astype(BF16)
            p_tab[u, M + 16 * a : M + 16 * a + 16, :] = (-(s * lc + c * ls)).astype(BF16)

    load.wait()
    q = q_out[...]
    over = (((1,), (1,)), ((), ()))
    from_real = lax.dot_general(x_buf[0], q, over, preferred_element_type=F32)
    from_imag = lax.dot_general(x_buf[1], q, over, preferred_element_type=F32)
    a_both = jnp.concatenate(
        [from_real[:, :M] - from_imag[:, M:], from_real[:, M:] + from_imag[:, :M]], 1
    ).astype(BF16)
    a_both = dot(a_both, perm[...]).astype(BF16)

    pl.semaphore_wait(barrier, TEAM + FACETS - 2)

    def partial(l, t):
        v = dot(p_tab[2 * t + l], a_both)
        return jnp.concatenate([v[:M, :M] - v[M:, M:], v[:M, M:] + v[M:, :M]], 1).astype(BF16)

    for l in range(PAIR):

        @pl.loop(1, TEAM)
        def _(i):
            t, to = mate(i)
            send1[l, i] = partial(l, t)
            pltpu.make_async_remote_copy(
                src_ref=send1.at[l, i], dst_ref=recv1.at[l, i], send_sem=s1.at[l, i], recv_sem=r1.at[l, i],
                device_id=to, device_id_type=MESH,
            ).start()

        recv1[l, 0] = partial(l, member)

    scale = 1.0 / math.sqrt(XM)
    place = (foff[mine, 0] + iota((16, M), 1)) & (XM - 1)
    lc, ls = cis(iota((16, M), 0) * place & (XM - 1), XM)
    lc, ls = lc * scale, ls * scale
    place = (foff[mine, 0] + iota((32, M), 1)) & (XM - 1)
    hc, hs = cis(16 * iota((32, M), 0) * place & (XM - 1), XM)
    for a in range(32):
        c, s = hc[a : a + 1], hs[a : a + 1]
        r_tab[16 * a : 16 * a + 16, :M] = (c * lc - s * ls).astype(BF16)
        r_tab[16 * a : 16 * a + 16, M:] = (s * lc + c * ls).astype(BF16)

    def waited(send, recv, i, l, ssem, rsem):
        return pltpu.make_async_remote_copy(
            src_ref=send.at[l, i], dst_ref=recv.at[l, i], send_sem=ssem.at[l, i], recv_sem=rsem.at[l, i],
            device_id=mate(1)[1], device_id_type=MESH,
        )

    def bulk(send, recv, l, ssem, rsem):
        some = pl.ds(0, FACETS - 1)
        return pltpu.make_async_remote_copy(
            src_ref=send.at[l, some], dst_ref=recv.at[l, some], send_sem=ssem.at[l], recv_sem=rsem.at[l],
            device_id=peer(1)[1], device_id_type=MESH,
        )

    def ship(send, recv, l, i, ssem, rsem):
        t, to = peer(i)
        pltpu.make_async_remote_copy(
            src_ref=send.at[l, t], dst_ref=recv.at[l, mine], send_sem=ssem.at[l], recv_sem=rsem.at[l],
            device_id=to, device_id_type=MESH,
        ).start()

    for l in range(PAIR):
        total = recv1[l, 0].astype(F32)
        for i in range(1, TEAM):
            waited(send1, recv1, i, l, s1, r1).wait_recv()
            total = total + recv1[l, i].astype(F32)
        total = total.astype(BF16)
        cr, ci = total[:, :M], total[:, M:]
        both = jnp.concatenate([jnp.concatenate([cr, ci], 1), jnp.concatenate([ci, -cr], 1)], 0)
        kk = dot(r_tab[...], both).astype(BF16)
        send2[l, :, 0] = kk[:, :M].reshape(FACETS, BLOCK, M)
        send2[l, :, 1] = kk[:, M:].reshape(FACETS, BLOCK, M)

        @pl.loop(1, FACETS)
        def _(i):
            ship(send2, recv2, l, i, s2, r2)

        recv2[l, mine] = send2[l, mine]

    c, s = cis(16 * iota((32, XM), 0) * iota((32, XM), 1) & (XM - 1), XM)
    lc, ls = cis(iota((16, XM), 0) * iota((16, XM), 1) & (XM - 1), XM)
    lc, ls = lc * scale, ls * scale
    for a in range(32):
        hc, hs = c[a : a + 1], s[a : a + 1]
        f_tab[16 * a : 16 * a + 16, :XM] = (hc * lc - hs * ls).astype(BF16)
        f_tab[16 * a : 16 * a + 16, XM:] = (hs * lc + hc * ls).astype(BF16)

    def tiles_of(f):
        o = foff[f, 1]
        lane = iota((BLOCK, M), 1)
        return (lax.shift_right_logical(o, 7) + jnp.where(lane < (o & (M - 1)), 1, 0)) & 3

    for l in range(PAIR):
        bulk(send2, recv2, l, s2, r2).wait_recv()

        def gather(f, acc):
            tile = tiles_of(f)
            got = [recv2[l, f, part].astype(F32) for part in range(2)]
            return tuple(
                acc[4 * part + t] + jnp.where(tile == t, got[part], 0.0) for part in range(2) for t in range(4)
            )

        zero = jnp.zeros((BLOCK, M), F32)
        acc = lax.fori_loop(0, FACETS, gather, (zero,) * 8)
        g = jnp.concatenate([jnp.concatenate(acc[:4], 1), jnp.concatenate(acc[4:], 1)], 0).astype(BF16)
        v = dot(g, f_tab[...])
        weight = weights[:, l, :]
        h_real = weight * (v[:BLOCK, :XM] + v[BLOCK:, XM:])
        h_imag = weight * (v[BLOCK:, :XM] - v[:BLOCK, XM:])
        spectra[:, l, 0, :] = h_real
        spectra[:, l, 1, :] = h_imag
        v = dot(jnp.concatenate([h_real, h_imag], 0).astype(BF16), f_tab[...])
        space = [v[:BLOCK, :XM] - v[BLOCK:, XM:], v[BLOCK:, :XM] + v[:BLOCK, XM:]]

        def window(f):
            tile = tiles_of(f)
            for part in range(2):
                cut = [space[part][:, M * t : M * t + M] for t in range(4)]
                low = jnp.where(tile == 1, cut[1], cut[0])
                high = jnp.where(tile == 3, cut[3], cut[2])
                send3[l, f, part] = jnp.where(tile < 2, low, high).astype(BF16)

        @pl.loop(1, FACETS)
        def _(i):
            window(peer(i)[0])
            ship(send3, recv3, l, i, s3, r3)

        window(mine)
        recv3[l, mine] = send3[l, mine]

    for l in range(PAIR):
        bulk(send3, recv3, l, s3, r3).wait_recv()
        rows = jnp.concatenate([recv3[l, :, 0].reshape(XM, M), recv3[l, :, 1].reshape(XM, M)], 1)
        u = dot_t(rows, r_tab[...])
        send4[l] = jnp.concatenate([u[:M, :M] - u[M:, M:], u[M:, :M] + u[:M, M:]], 1).astype(BF16)

        @pl.loop(1, TEAM)
        def _(i):
            pltpu.make_async_remote_copy(
                src_ref=send4.at[l], dst_ref=recv4.at[l, i], send_sem=s4.at[l, i], recv_sem=r4.at[l, i],
                device_id=mate(i)[1], device_id_type=MESH,
            ).start()

        recv4[l, 0] = send4[l]

    def spread(l, i):
        d = recv4[l, i]
        d = jnp.concatenate([d, jnp.concatenate([d[:, M:], -d[:, :M]], 1)], 0)
        t = lax.rem(member - i + TEAM, TEAM)
        return dot(d, p_tab[2 * t + l])

    e = spread(0, 0) + spread(1, 0)
    for l in range(PAIR):
        for i in range(1, TEAM):
            pltpu.make_async_remote_copy(
                src_ref=send4.at[l], dst_ref=recv4.at[l, i], send_sem=s4.at[l, i], recv_sem=r4.at[l, i],
                device_id=mate(1)[1], device_id_type=MESH,
            ).wait_recv()
            e = e + spread(l, i)
    et_out[...] = dot(perm[...], e.astype(BF16)).astype(BF16)

    for l in range(PAIR):
        bulk(send2, recv2, l, s2, r2).wait_send()
        bulk(send3, recv3, l, s3, r3).wait_send()
        for i in range(1, TEAM):
            waited(send1, recv1, i, l, s1, r1).wait_send()
            pltpu.make_async_remote_copy(
                src_ref=send4.at[l], dst_ref=recv4.at[l, i], send_sem=s4.at[l, i], recv_sem=r4.at[l, i],
                device_id=mate(1)[1], device_id_type=MESH,
            ).wait_send()


def correction(et, q, out):
    gain = 2.0 * math.sqrt(YF / M)
    e = et[...]
    out[0, 0] = (dot_t(e, q[...]) * gain).astype(BF16)
    out[0, 1] = (dot_t(jnp.concatenate([e[M:], -e[:M]], 0), q[...]) * gain).astype(BF16)


def shards(facets, weights, facet_offsets, subgrid_offsets, column):
    smem = pl.BlockSpec(memory_space=pltpu.SMEM)
    vmem = pl.BlockSpec(memory_space=pltpu.VMEM)
    dma = pltpu.SemaphoreType.DMA
    et, q, spectra = pl.pallas_call(
        round_trip,
        out_shape=(
            jax.ShapeDtypeStruct((2 * M, ROWS), BF16),
            jax.ShapeDtypeStruct((2 * M, YF), BF16),
            jax.ShapeDtypeStruct((BLOCK, PAIR, 2, XM), F32),
        ),
        in_specs=[pl.BlockSpec(memory_space=pl.ANY), vmem, smem, smem, smem],
        out_specs=(vmem, vmem, vmem),
        scratch_shapes=[
            pltpu.VMEM((2, ROWS, YF), BF16),
            pltpu.VMEM((8, YF), F32),
            pltpu.VMEM((8, YF), F32),
            pltpu.VMEM((16, YF), F32),
            pltpu.VMEM((16, YF), F32),
            pltpu.VMEM((SUBS, 2 * M, ROWS), BF16),
            pltpu.VMEM((XM, 2 * XM), BF16),
            pltpu.VMEM((XM, 2 * M), BF16),
            pltpu.VMEM((2 * M, 2 * M), BF16),
            pltpu.VMEM((PAIR, TEAM, M, 2 * M), BF16),
            pltpu.VMEM((PAIR, TEAM, M, 2 * M), BF16),
            pltpu.VMEM((PAIR, FACETS, 2, BLOCK, M), BF16),
            pltpu.VMEM((PAIR, FACETS, 2, BLOCK, M), BF16),
            pltpu.VMEM((PAIR, FACETS, 2, BLOCK, M), BF16),
            pltpu.VMEM((PAIR, FACETS, 2, BLOCK, M), BF16),
            pltpu.VMEM((PAIR, M, 2 * M), BF16),
            pltpu.VMEM((PAIR, TEAM, M, 2 * M), BF16),
            dma,
            dma((PAIR, TEAM)), dma((PAIR, TEAM)),
            dma((PAIR,)), dma((PAIR,)),
            dma((PAIR,)), dma((PAIR,)),
            dma((PAIR, TEAM)), dma((PAIR, TEAM)),
        ],
        compiler_params=pltpu.CompilerParams(
            collective_id=0, has_side_effects=True, vmem_limit_bytes=40 * 2**20
        ),
        cost_estimate=pl.CostEstimate(flops=3 * 10**9, bytes_accessed=4 * 10**6, transcendentals=0),
        name="round_trip",
    )(facets[0], weights, facet_offsets, subgrid_offsets, column)
    part = 512
    update = pl.pallas_call(
        correction,
        grid=(YF // part,),
        out_shape=jax.ShapeDtypeStruct((1, 2, ROWS, YF), BF16),
        in_specs=[
            pl.BlockSpec((2 * M, ROWS), lambda i: (0, 0)),
            pl.BlockSpec((2 * M, part), lambda i: (0, i)),
        ],
        out_specs=pl.BlockSpec((1, 2, ROWS, part), lambda i: (0, 0, 0, i)),
        name="correction",
    )(et, q)
    return update, spectra


def solution(mesh):
    return jax.shard_map(
        shards,
        mesh=mesh,
        in_specs=(
            P("facet", None, ("half", "sub"), None),
            P("facet", ("half", "sub"), None),
            P(),
            P(),
            P(),
        ),
        out_specs=(
            P("facet", None, ("half", "sub"), None),
            P("facet", ("half", "sub"), None, None),
        ),
        check_vma=False,
    )
```

```python
import functools
import math

import jax
import jax.numpy as jnp
from jax import lax
from jax.experimental import pallas as pl
from jax.experimental.pallas import tpu as pltpu
from jax.sharding import PartitionSpec as P

YF = 2048
M = 128
XM = 512
SUBS = 16
FACETS = 32
PAIR = 2
ROWS = 256
BLOCK = 16
VMEM_MIB = 60
MESH = pl.DeviceIdType.MESH
F32 = jnp.float32
BF16 = jnp.bfloat16


def cis(turn, n):
    quarter = n // 4
    q = lax.shift_right_logical(turn + n // 8, quarter.bit_length() - 1)
    x = (turn - q * quarter).astype(F32) * (2.0 * math.pi / n)
    z = x * x
    s = x + x * z * (-1.6666654611e-1 + z * (8.3321608736e-3 - 1.9515295891e-4 * z))
    c = 1.0 - 0.5 * z + z * z * (4.166664568298827e-2 + z * (-1.388731625493765e-3 + 2.443315711809948e-5 * z))
    swap = (q & 1) == 1
    cosine = jnp.where(swap, s, c)
    sine = jnp.where(swap, c, s)
    cosine = jnp.where(((q + 1) & 2) != 0, -cosine, cosine)
    sine = jnp.where((q & 2) != 0, -sine, sine)
    return cosine, sine


def iota(shape, dim):
    return lax.broadcasted_iota(jnp.int32, shape, dim)


def taper(pos):
    _, s = cis(2 * pos + 1, 4 * YF)
    return s * s * (1.0 / math.sqrt(YF))


def dot(a, b):
    return jnp.dot(a, b, preferred_element_type=F32)


def dot_t(a, b):
    return lax.dot_general(a, b, (((0,), (0,)), ((), ())), preferred_element_type=F32)


def remote(src, dst, send, recv, to):
    return pltpu.make_async_remote_copy(
        src_ref=src, dst_ref=dst, send_sem=send, recv_sem=recv, device_id=to, device_id_type=MESH
    )


def round_trip(
    facets, weights, foff_in, soff_in, col_in,
    et_out, q_out, spectra,
    foff, soff, col, x_buf, w_buf, hi_c, hi_s, lo_c, lo_s, p_tab, f_tab, r_tab, perm,
    a_buf, send1, recv1, send2, mid2, recv2, recv3, win3, rows3, recv4, send5, recv5,
    small_sem, x_sem, w_sem, sa, ra, s1, r1, s2, r2, sz2, rz2, sz3, rz3, s3, r3, s4, r4, s5, r5,
):
    mine = lax.axis_index("facet")
    x = lax.axis_index("half")
    hi = lax.axis_index("sub")
    core = lax.rem(mine, 2)
    z = lax.rem(mine // 2, 8)
    low = mine // 16
    slot = low * 2 + core

    def at_x(d):
        return {"half": lax.rem(x + d, 4)}

    def at_z(d):
        return {"facet": low * 16 + lax.rem(z + d, 8) * 2 + core}

    def slot_of(q):
        return lax.rem(low + q // 2, 2) * 2 + lax.rem(core + q % 2, 2)

    def at_slot(q):
        return {"facet": lax.rem(low + q // 2, 2) * 16 + z * 2 + lax.rem(core + q % 2, 2)}

    across = {"sub": 1 - hi}

    smalls = [
        pltpu.make_async_copy(src, dst, small_sem.at[i])
        for i, (src, dst) in enumerate([(col_in, col), (foff_in, foff), (soff_in, soff)])
    ]
    for copy in smalls:
        copy.start()
    load = pltpu.make_async_copy(facets.at[0], x_buf, x_sem)
    load.start()
    load_w = pltpu.make_async_copy(weights, w_buf, w_sem)
    load_w.start()

    barrier = pltpu.get_barrier_semaphore()
    friends = [across] + [at_x(d) for d in (1, 2, 3)] + [at_slot(q) for q in (1, 2, 3)] + [at_z(d) for d in range(1, 8)]
    for to in friends:
        pl.semaphore_signal(barrier, inc=1, device_id=to, device_id_type=MESH)

    y = iota((8, YF), 1)
    c, s = cis(iota((16, YF), 0) * iota((16, YF), 1) & (YF - 1), YF)
    w = taper(iota((1, YF), 1))
    lo_c[...] = c * w
    lo_s[...] = s * w
    for copy in smalls:
        copy.wait()
    c, s = cis(((col[0] + 16 * iota((8, YF), 0)) & (YF - 1)) * y & (YF - 1), YF)
    hi_c[...] = c
    hi_s[...] = s

    @pl.loop(0, 8)
    def _(a):
        hc, hs = hi_c[pl.ds(a, 1), :], hi_s[pl.ds(a, 1), :]
        lc, ls = lo_c[...], lo_s[...]
        at = pl.multiple_of(a * 16, 16)
        q_out[pl.ds(at, 16), :] = (hc * lc - hs * ls).astype(BF16)
        q_out[pl.ds(at + M, 16), :] = (-(hs * lc + hc * ls)).astype(BF16)

    turn = foff[1, mine] & (M - 1)
    k, c = iota((2 * M, 2 * M), 0), iota((2 * M, 2 * M), 1)
    same = ((k & (M - 1)) == ((c - turn) & (M - 1))) & ((k < M) == (c < M))
    perm[...] = jnp.where(same, 1.0, 0.0).astype(BF16)

    load.wait()
    q = q_out[...]
    over = (((1,), (1,)), ((), ()))
    from_real = lax.dot_general(x_buf[0], q, over, preferred_element_type=F32)
    from_imag = lax.dot_general(x_buf[1], q, over, preferred_element_type=F32)
    a_both = jnp.concatenate(
        [from_real[:, :M] - from_imag[:, M:], from_real[:, M:] + from_imag[:, :M]], 1
    ).astype(BF16)
    a_buf[hi] = dot(a_both, perm[...]).astype(BF16)

    pl.semaphore_wait(barrier, len(friends))
    swap_a = remote(a_buf.at[hi], a_buf.at[hi], sa, ra, across)
    swap_a.start()

    first = x * (2 * ROWS)
    pos = first + iota((16, 2 * ROWS), 1)
    c, s = cis(iota((16, 2 * ROWS), 0) * pos & (YF - 1), YF)
    w = taper(first + iota((1, 2 * ROWS), 1))
    lc, ls = c * w, s * w

    @pl.loop(0, 2 * 4)
    def _(u):
        freq = (soff[4 * (u // 2) + 2 * hi + lax.rem(u, 2)] + 16 * iota((8, 2 * ROWS), 0)) & (YF - 1)
        hc, hs = cis(freq * (first + iota((8, 2 * ROWS), 1)) & (YF - 1), YF)
        for a in range(8):
            c, s = hc[a : a + 1], hs[a : a + 1]
            real = (c * lc - s * ls).astype(BF16)
            imag = (-(s * lc + c * ls)).astype(BF16)
            for b in range(2):
                p_tab[b, u, 16 * a : 16 * a + 16, :] = real[:, ROWS * b : ROWS * b + ROWS]
                p_tab[b, u, M + 16 * a : M + 16 * a + 16, :] = imag[:, ROWS * b : ROWS * b + ROWS]

    def partial(l, to_x):
        u = 2 * to_x + l
        v = dot(p_tab[0, u], a_buf[0]) + dot(p_tab[1, u], a_buf[1])
        return jnp.concatenate([v[:M, :M] - v[M:, M:], v[:M, M:] + v[M:, :M]], 1).astype(BF16)

    swap_a.wait()
    for l in range(PAIR):
        for d in (2, 1, 3):
            send1[l, d] = partial(l, lax.rem(x + d, 4))
            remote(send1.at[l, d], recv1.at[l, d], s1.at[l, d], r1.at[l, d], at_x(d)).start()
        recv1[l, 0] = partial(l, x)

    scale = 1.0 / math.sqrt(XM)
    place = (foff[0, mine] + iota((16, M), 1)) & (XM - 1)
    lc, ls = cis(iota((16, M), 0) * place & (XM - 1), XM)
    lc, ls = lc * scale, ls * scale
    place = (foff[0, mine] + iota((32, M), 1)) & (XM - 1)
    i = iota((32, M), 0)
    block = (i & 16) + 2 * (i & 7) + (lax.shift_right_logical(i, 3) & 1)
    hc, hs = cis(16 * block * place & (XM - 1), XM)
    for a in range(32):
        c, s = hc[a : a + 1], hs[a : a + 1]
        r_tab[16 * a : 16 * a + 16, :M] = (c * lc - s * ls).astype(BF16)
        r_tab[16 * a : 16 * a + 16, M:] = (s * lc + c * ls).astype(BF16)

    c, s = cis(16 * iota((32, XM), 0) * iota((32, XM), 1) & (XM - 1), XM)
    lc, ls = cis(iota((16, XM), 0) * iota((16, XM), 1) & (XM - 1), XM)
    lc, ls = lc * scale, ls * scale
    for a in range(32):
        hc, hs = c[a : a + 1], s[a : a + 1]
        f_tab[16 * a : 16 * a + 16, :XM] = (hc * lc - hs * ls).astype(BF16)
        f_tab[16 * a : 16 * a + 16, XM:] = (hs * lc + hc * ls).astype(BF16)

    far = (4, 3, 5, 2, 6, 1, 7)
    near = (1, 7, 2, 6, 3, 5, 4)

    for l in range(PAIR):
        total = recv1[l, 0].astype(F32)
        for d in (1, 3, 2):
            remote(send1.at[l, d], recv1.at[l, d], s1.at[l, d], r1.at[l, d], at_x(d)).wait_recv()
            total = total + recv1[l, d].astype(F32)
        total = total.astype(BF16)
        cr, ci = total[:, :M], total[:, M:]
        both = jnp.concatenate([jnp.concatenate([cr, ci], 1), jnp.concatenate([ci, -cr], 1)], 0)
        kk = dot(r_tab[...], both).astype(BF16)
        send2[l, :, :, 0] = kk[:, :M].reshape(4, 8, BLOCK, M)
        send2[l, :, :, 1] = kk[:, M:].reshape(4, 8, BLOCK, M)
        for q in (3, 2, 1):
            remote(send2.at[l, slot_of(q)], mid2.at[l, slot], s2.at[l, q], r2.at[l, q], at_slot(q)).start()
        mid2[l, slot] = send2[l, slot]

    def z2(l, d):
        return remote(
            mid2.at[l, :, lax.rem(z + d, 8)], recv2.at[l, z], sz2.at[l, d], rz2.at[l, d], at_z(d)
        )

    for l in range(PAIR):
        for q in (1, 2, 3):
            remote(send2.at[l, slot_of(q)], mid2.at[l, slot_of(q)], s2.at[l, q], r2.at[l, q], at_slot(q)).wait_recv()
        for d in far:
            z2(l, d).start()

    lane = iota((BLOCK, M), 1)

    def tiles_of(f):
        o = foff[1, f]
        return (lax.shift_right_logical(o, 7) + jnp.where(lane < (o & (M - 1)), 1, 0)) & 3

    load_w.wait()
    for l in range(PAIR):
        acc = [[jnp.zeros((BLOCK, M), F32) for _ in range(4)] for _ in range(2)]
        for d in (0,) + near:
            from_z = lax.rem(z + 8 - d, 8)
            if d:
                remote(recv2.at[l, from_z], recv2.at[l, from_z], sz2.at[l, d], rz2.at[l, d], at_z(d)).wait_recv()
            for q in range(4):
                tile = tiles_of((q // 2) * 16 + from_z * 2 + q % 2)
                for part in range(2):
                    got = (recv2[l, from_z, q, part] if d else mid2[l, q, z, part]).astype(F32)
                    for t in range(4):
                        acc[part][t] = acc[part][t] + jnp.where(tile == t, got, 0.0)
        g = jnp.concatenate([jnp.concatenate(acc[0], 1), jnp.concatenate(acc[1], 1)], 0).astype(BF16)
        v = dot(g, f_tab[...])
        weight = w_buf[:, l, :]
        h_real = weight * (v[:BLOCK, :XM] + v[BLOCK:, XM:])
        h_imag = weight * (v[BLOCK:, :XM] - v[:BLOCK, XM:])
        v = dot(jnp.concatenate([h_real, h_imag], 0).astype(BF16), f_tab[...])
        recv3[l, z, 0] = (v[:BLOCK, :XM] - v[BLOCK:, XM:]).astype(BF16)
        recv3[l, z, 1] = (v[BLOCK:, :XM] + v[:BLOCK, XM:]).astype(BF16)
        for d in far:
            remote(recv3.at[l, z], recv3.at[l, z], sz3.at[l, d], rz3.at[l, d], at_z(d)).start()
        spectra[:, l, 0, :] = h_real
        spectra[:, l, 1, :] = h_imag

    for l in range(PAIR):
        tiles = [tiles_of(lax.rem(low + q // 2, 2) * 16 + z * 2 + lax.rem(core + q % 2, 2)) for q in range(4)]
        for d in (0,) + near:
            from_z = lax.rem(z + 8 - d, 8)
            if d:
                remote(recv3.at[l, from_z], recv3.at[l, from_z], sz3.at[l, d], rz3.at[l, d], at_z(d)).wait_recv()
            for part in range(2):
                whole = recv3[l, from_z, part].astype(F32)
                cut = [whole[:, M * t : M * t + M] for t in range(4)]
                for q in range(4):
                    one = jnp.where(tiles[q] == 1, cut[1], cut[0])
                    two = jnp.where(tiles[q] == 3, cut[3], cut[2])
                    one = jnp.where(tiles[q] < 2, one, two).astype(BF16)
                    if q:
                        win3[l, q, from_z, part] = one
                    else:
                        rows3[l, slot, from_z, part] = one
        for q in (3, 2, 1):
            remote(win3.at[l, q], rows3.at[l, slot], s3.at[l, q], r3.at[l, q], at_slot(q)).start()

    e_here = e_there = None
    for l in range(PAIR):
        for q in (1, 2, 3):
            remote(win3.at[l, q], rows3.at[l, slot_of(q)], s3.at[l, q], r3.at[l, q], at_slot(q)).wait_recv()
        rows = jnp.concatenate([rows3[l, :, :, 0].reshape(XM, M), rows3[l, :, :, 1].reshape(XM, M)], 1)
        u = dot_t(rows, r_tab[...])
        recv4[l, x] = jnp.concatenate([u[:M, :M] - u[M:, M:], u[M:, :M] + u[:M, M:]], 1).astype(BF16)
        for d in (2, 1, 3):
            remote(recv4.at[l, x], recv4.at[l, x], s4.at[l, d], r4.at[l, d], at_x(d)).start()

    for l in range(PAIR):
        for d in (0, 1, 3, 2):
            from_x = lax.rem(x + 4 - d, 4)
            if d:
                remote(recv4.at[l, from_x], recv4.at[l, from_x], s4.at[l, d], r4.at[l, d], at_x(d)).wait_recv()
            v = recv4[l, from_x]
            v = jnp.concatenate([v, jnp.concatenate([v[:, M:], -v[:, :M]], 1)], 0)
            there = dot(v, p_tab[1 - hi, 2 * from_x + l])
            here = dot(v, p_tab[hi, 2 * from_x + l])
            e_there = there if e_there is None else e_there + there
            e_here = here if e_here is None else e_here + here
    send5[...] = e_there.astype(BF16)
    swap_e = remote(send5, recv5, s5, r5, across)
    swap_e.start()
    swap_e.wait_recv()
    e = (e_here + recv5[...].astype(F32)).astype(BF16)
    et_out[...] = dot(perm[...], e).astype(BF16)

    swap_e.wait_send()
    for l in range(PAIR):
        for d in range(1, 4):
            remote(send1.at[l, d], recv1.at[l, d], s1.at[l, d], r1.at[l, d], at_x(d)).wait_send()
            remote(recv4.at[l, x], recv4.at[l, x], s4.at[l, d], r4.at[l, d], at_x(d)).wait_send()
            remote(send2.at[l, slot_of(d)], mid2.at[l, slot], s2.at[l, d], r2.at[l, d], at_slot(d)).wait_send()
            remote(win3.at[l, d], rows3.at[l, slot], s3.at[l, d], r3.at[l, d], at_slot(d)).wait_send()
        for d in range(1, 8):
            z2(l, d).wait_send()
            remote(recv3.at[l, z], recv3.at[l, z], sz3.at[l, d], rz3.at[l, d], at_z(d)).wait_send()


def correction(et, q, spectra_in, out, spectra, buf, sems, sem):
    copy = pltpu.make_async_copy(spectra_in, spectra, sem)
    copy.start()
    gain = 2.0 * math.sqrt(YF / M)
    real = et[...]
    imag = jnp.concatenate([real[M:], -real[:M]], 0)
    parts = buf.shape[0]
    width = buf.shape[3]
    moves = []
    for i in range(parts):
        table = q[:, width * i : width * i + width]
        buf[i, 0] = (dot_t(real, table) * gain).astype(BF16)
        buf[i, 1] = (dot_t(imag, table) * gain).astype(BF16)
        move = pltpu.make_async_copy(buf.at[i], out.at[0, :, :, pl.ds(width * i, width)], sems.at[i])
        move.start()
        moves.append(move)
    for move in moves:
        move.wait()
    copy.wait()


def shards(facets, weights, facet_offsets, subgrid_offsets, column):
    hbm = pl.BlockSpec(memory_space=pl.ANY)
    vmem = pl.BlockSpec(memory_space=pltpu.VMEM)
    dma = pltpu.SemaphoreType.DMA
    pair_of = lambda *shape: pltpu.VMEM((PAIR, *shape), BF16)
    et, q, spectra = pl.pallas_call(
        round_trip,
        out_shape=(
            jax.ShapeDtypeStruct((2 * M, ROWS), BF16),
            jax.ShapeDtypeStruct((2 * M, YF), BF16),
            jax.ShapeDtypeStruct((BLOCK, PAIR, 2, XM), F32),
        ),
        in_specs=[hbm] * 5,
        out_specs=(vmem, vmem, vmem),
        scratch_shapes=[
            pltpu.SMEM((2, FACETS), jnp.int32),
            pltpu.SMEM((SUBS,), jnp.int32),
            pltpu.SMEM((1,), jnp.int32),
            pltpu.VMEM((2, ROWS, YF), BF16),
            pltpu.VMEM((BLOCK, PAIR, XM), F32),
            pltpu.VMEM((8, YF), F32),
            pltpu.VMEM((8, YF), F32),
            pltpu.VMEM((16, YF), F32),
            pltpu.VMEM((16, YF), F32),
            pltpu.VMEM((2, 8, 2 * M, ROWS), BF16),
            pltpu.VMEM((XM, 2 * XM), BF16),
            pltpu.VMEM((XM, 2 * M), BF16),
            pltpu.VMEM((2 * M, 2 * M), BF16),
            pltpu.VMEM((2, ROWS, 2 * M), BF16),
            pair_of(4, M, 2 * M),
            pair_of(4, M, 2 * M),
            pair_of(4, 8, 2, BLOCK, M),
            pair_of(4, 8, 2, BLOCK, M),
            pair_of(8, 4, 2, BLOCK, M),
            pair_of(8, 2, BLOCK, XM),
            pair_of(4, 8, 2, BLOCK, M),
            pair_of(4, 8, 2, BLOCK, M),
            pair_of(4, M, 2 * M),
            pltpu.VMEM((2 * M, ROWS), BF16),
            pltpu.VMEM((2 * M, ROWS), BF16),
            dma((3,)), dma, dma,
            dma, dma,
            dma((PAIR, 4)), dma((PAIR, 4)),
            dma((PAIR, 4)), dma((PAIR, 4)),
            dma((PAIR, 8)), dma((PAIR, 8)),
            dma((PAIR, 8)), dma((PAIR, 8)),
            dma((PAIR, 4)), dma((PAIR, 4)),
            dma((PAIR, 4)), dma((PAIR, 4)),
            dma, dma,
        ],
        compiler_params=pltpu.CompilerParams(
            collective_id=0, has_side_effects=True, vmem_limit_bytes=VMEM_MIB * 2**20
        ),
        cost_estimate=pl.CostEstimate(flops=3 * 10**9, bytes_accessed=4 * 10**6, transcendentals=0),
        name="round_trip",
    )(facets, weights, facet_offsets.T, subgrid_offsets, column)
    parts = 4
    update, spectra = pl.pallas_call(
        correction,
        out_shape=(
            jax.ShapeDtypeStruct((1, 2, ROWS, YF), BF16),
            jax.ShapeDtypeStruct((BLOCK, PAIR, 2, XM), F32),
        ),
        in_specs=[vmem, vmem, hbm],
        out_specs=(hbm, hbm),
        scratch_shapes=[
            pltpu.VMEM((parts, 2, ROWS, YF // parts), BF16),
            dma((parts,)),
            dma,
        ],
        compiler_params=pltpu.CompilerParams(vmem_limit_bytes=24 * 2**20),
        cost_estimate=pl.CostEstimate(flops=10**9, bytes_accessed=3 * 10**6, transcendentals=0),
        name="correction",
    )(et, q, spectra)
    return update, spectra


def solution(mesh):
    return jax.shard_map(
        shards,
        mesh=mesh,
        in_specs=(
            P("facet", None, ("half", "sub"), None),
            P("facet", ("half", "sub"), None),
            P(),
            P(),
            P(),
        ),
        out_specs=(
            P("facet", None, ("half", "sub"), None),
            P("facet", ("half", "sub"), None, None),
        ),
        check_vma=False,
    )
```

```python
import functools
import math

import jax
import jax.numpy as jnp
from jax import lax
from jax.experimental import pallas as pl
from jax.experimental.pallas import tpu as pltpu
from jax.sharding import PartitionSpec as P

YF = 2048
M = 128
XM = 512
SUBS = 16
FACETS = 32
PAIR = 2
ROWS = 256
BLOCK = 16
VMEM_MIB = 60
MESH = pl.DeviceIdType.MESH
F32 = jnp.float32
BF16 = jnp.bfloat16


def cis(turn, n):
    quarter = n // 4
    q = lax.shift_right_logical(turn + n // 8, quarter.bit_length() - 1)
    x = (turn - q * quarter).astype(F32) * (2.0 * math.pi / n)
    z = x * x
    s = x + x * z * (-1.6666654611e-1 + z * (8.3321608736e-3 - 1.9515295891e-4 * z))
    c = 1.0 - 0.5 * z + z * z * (4.166664568298827e-2 + z * (-1.388731625493765e-3 + 2.443315711809948e-5 * z))
    swap = (q & 1) == 1
    cosine = jnp.where(swap, s, c)
    sine = jnp.where(swap, c, s)
    cosine = jnp.where(((q + 1) & 2) != 0, -cosine, cosine)
    sine = jnp.where((q & 2) != 0, -sine, sine)
    return cosine, sine


def iota(shape, dim):
    return lax.broadcasted_iota(jnp.int32, shape, dim)


def taper(pos):
    _, s = cis(2 * pos + 1, 4 * YF)
    return s * s * (1.0 / math.sqrt(YF))


def dot(a, b):
    return jnp.dot(a, b, preferred_element_type=F32)


def dot_t(a, b):
    return lax.dot_general(a, b, (((0,), (0,)), ((), ())), preferred_element_type=F32)


def remote(src, dst, send, recv, to):
    return pltpu.make_async_remote_copy(
        src_ref=src, dst_ref=dst, send_sem=send, recv_sem=recv, device_id=to, device_id_type=MESH
    )


def round_trip(
    facets, weights, foff_in, soff_in, col_in,
    et_hbm, q_hbm, spectra_hbm,
    et_out, q_out, spectra, foff, soff, col, x_buf, w_buf, hi_c, hi_s, lo_c, lo_s, p_tab, f_tab, r_tab, perm,
    a_buf, send1, recv1, send2, mid2, ring, got2, recv3, win3, rows3, recv4, send5, recv5,
    out_sem, small_sem, x_sem, w_sem, sa, ra, s1, r1, s2, r2, sz2, rz2, sz3, rz3, s3, r3, s4, r4, s5, r5,
):
    mine = lax.axis_index("facet")
    x = lax.axis_index("half")
    hi = lax.axis_index("sub")
    core = lax.rem(mine, 2)
    z = lax.rem(mine // 2, 8)
    low = mine // 16
    slot = low * 2 + core

    def at_x(d):
        return {"half": lax.rem(x + d, 4)}

    def at_z(d):
        return {"facet": low * 16 + lax.rem(z + d, 8) * 2 + core}

    def slot_of(q):
        return lax.rem(low + q // 2, 2) * 2 + lax.rem(core + q % 2, 2)

    def at_slot(q):
        return {"facet": lax.rem(low + q // 2, 2) * 16 + z * 2 + lax.rem(core + q % 2, 2)}

    across = {"sub": 1 - hi}

    smalls = [
        pltpu.make_async_copy(src, dst, small_sem.at[i])
        for i, (src, dst) in enumerate([(col_in, col), (foff_in, foff), (soff_in, soff)])
    ]
    for copy in smalls:
        copy.start()
    load = pltpu.make_async_copy(facets.at[0], x_buf, x_sem)
    load.start()
    load_w = pltpu.make_async_copy(weights, w_buf, w_sem)
    load_w.start()

    barrier = pltpu.get_barrier_semaphore()
    friends = [across] + [at_x(d) for d in (1, 2, 3)] + [at_slot(q) for q in (1, 2, 3)] + [at_z(1), at_z(7)]
    for to in friends:
        pl.semaphore_signal(barrier, inc=1, device_id=to, device_id_type=MESH)

    y = iota((8, YF), 1)
    c, s = cis(iota((16, YF), 0) * iota((16, YF), 1) & (YF - 1), YF)
    w = taper(iota((1, YF), 1))
    lo_c[...] = c * w
    lo_s[...] = s * w
    for copy in smalls:
        copy.wait()
    c, s = cis(((col[0] + 16 * iota((8, YF), 0)) & (YF - 1)) * y & (YF - 1), YF)
    hi_c[...] = c
    hi_s[...] = s

    @pl.loop(0, 8)
    def _(a):
        hc, hs = hi_c[pl.ds(a, 1), :], hi_s[pl.ds(a, 1), :]
        lc, ls = lo_c[...], lo_s[...]
        at = pl.multiple_of(a * 16, 16)
        q_out[pl.ds(at, 16), :] = (hc * lc - hs * ls).astype(BF16)
        q_out[pl.ds(at + M, 16), :] = (-(hs * lc + hc * ls)).astype(BF16)

    store_q = pltpu.make_async_copy(q_out, q_hbm, out_sem.at[0])
    store_q.start()

    turn = foff[1, mine] & (M - 1)
    k, c = iota((2 * M, 2 * M), 0), iota((2 * M, 2 * M), 1)
    same = ((k & (M - 1)) == ((c - turn) & (M - 1))) & ((k < M) == (c < M))
    perm[...] = jnp.where(same, 1.0, 0.0).astype(BF16)

    load.wait()
    q = q_out[...]
    over = (((1,), (1,)), ((), ()))
    from_real = lax.dot_general(x_buf[0], q, over, preferred_element_type=F32)
    from_imag = lax.dot_general(x_buf[1], q, over, preferred_element_type=F32)
    a_both = jnp.concatenate(
        [from_real[:, :M] - from_imag[:, M:], from_real[:, M:] + from_imag[:, :M]], 1
    ).astype(BF16)
    a_buf[hi] = dot(a_both, perm[...]).astype(BF16)

    pl.semaphore_wait(barrier, len(friends))
    swap_a = remote(a_buf.at[hi], a_buf.at[hi], sa, ra, across)
    swap_a.start()

    first = x * (2 * ROWS)
    pos = first + iota((16, 2 * ROWS), 1)
    c, s = cis(iota((16, 2 * ROWS), 0) * pos & (YF - 1), YF)
    w = taper(first + iota((1, 2 * ROWS), 1))
    lc, ls = c * w, s * w

    @pl.loop(0, 2 * 4)
    def _(u):
        freq = (soff[4 * (u // 2) + 2 * hi + lax.rem(u, 2)] + 16 * iota((8, 2 * ROWS), 0)) & (YF - 1)
        hc, hs = cis(freq * (first + iota((8, 2 * ROWS), 1)) & (YF - 1), YF)
        for a in range(8):
            c, s = hc[a : a + 1], hs[a : a + 1]
            real = (c * lc - s * ls).astype(BF16)
            imag = (-(s * lc + c * ls)).astype(BF16)
            for b in range(2):
                p_tab[b, u, 16 * a : 16 * a + 16, :] = real[:, ROWS * b : ROWS * b + ROWS]
                p_tab[b, u, M + 16 * a : M + 16 * a + 16, :] = imag[:, ROWS * b : ROWS * b + ROWS]

    def partial(l, to_x):
        u = 2 * to_x + l
        v = dot(p_tab[0, u], a_buf[0]) + dot(p_tab[1, u], a_buf[1])
        return jnp.concatenate([v[:M, :M] - v[M:, M:], v[:M, M:] + v[M:, :M]], 1).astype(BF16)

    swap_a.wait()
    for l in range(PAIR):
        for d in (2, 1, 3):
            send1[l, d] = partial(l, lax.rem(x + d, 4))
            remote(send1.at[l, d], recv1.at[l, d], s1.at[l, d], r1.at[l, d], at_x(d)).start()
        recv1[l, 0] = partial(l, x)

    scale = 1.0 / math.sqrt(XM)
    place = (foff[0, mine] + iota((16, M), 1)) & (XM - 1)
    lc, ls = cis(iota((16, M), 0) * place & (XM - 1), XM)
    lc, ls = lc * scale, ls * scale
    place = (foff[0, mine] + iota((32, M), 1)) & (XM - 1)
    i = iota((32, M), 0)
    block = (i & 16) + 2 * (i & 7) + (lax.shift_right_logical(i, 3) & 1)
    hc, hs = cis(16 * block * place & (XM - 1), XM)
    for a in range(32):
        c, s = hc[a : a + 1], hs[a : a + 1]
        r_tab[16 * a : 16 * a + 16, :M] = (c * lc - s * ls).astype(BF16)
        r_tab[16 * a : 16 * a + 16, M:] = (s * lc + c * ls).astype(BF16)

    c, s = cis(16 * iota((32, XM), 0) * iota((32, XM), 1) & (XM - 1), XM)
    lc, ls = cis(iota((16, XM), 0) * iota((16, XM), 1) & (XM - 1), XM)
    lc, ls = lc * scale, ls * scale
    for a in range(32):
        hc, hs = c[a : a + 1], s[a : a + 1]
        f_tab[16 * a : 16 * a + 16, :XM] = (hc * lc - hs * ls).astype(BF16)
        f_tab[16 * a : 16 * a + 16, XM:] = (hs * lc + hc * ls).astype(BF16)

    for l in range(PAIR):
        total = recv1[l, 0].astype(F32)
        for d in (1, 3, 2):
            remote(send1.at[l, d], recv1.at[l, d], s1.at[l, d], r1.at[l, d], at_x(d)).wait_recv()
            total = total + recv1[l, d].astype(F32)
        total = total.astype(BF16)
        cr, ci = total[:, :M], total[:, M:]
        both = jnp.concatenate([jnp.concatenate([cr, ci], 1), jnp.concatenate([ci, -cr], 1)], 0)
        kk = dot(r_tab[...], both).astype(BF16)
        send2[l, :, :, 0] = kk[:, :M].reshape(4, 8, BLOCK, M)
        send2[l, :, :, 1] = kk[:, M:].reshape(4, 8, BLOCK, M)
        for q in (3, 2, 1):
            remote(send2.at[l, slot_of(q)], mid2.at[l, slot], s2.at[l, q], r2.at[l, q], at_slot(q)).start()
        mid2[l, slot] = send2[l, slot]

    lane = iota((BLOCK, M), 1)

    def tiles_of(f):
        o = foff[1, f]
        return (lax.shift_right_logical(o, 7) + jnp.where(lane < (o & (M - 1)), 1, 0)) & 3

    def hops(l, way):
        return 4 if l == way else 3

    def on(way, count):
        return lax.rem(z + (count if way == 0 else 8 - count), 8)

    def onward(way):
        return at_z(1 if way == 0 else 7)

    chains = [(l, way) for l in range(PAIR) for way in range(2)]
    own_tiles = [tiles_of((q // 2) * 16 + z * 2 + q % 2) for q in range(4)]

    def placed(l, to_z, part):
        acc = [jnp.zeros((BLOCK, M), F32) for _ in range(4)]
        for q in range(4):
            value = mid2[l, q, to_z, part].astype(F32)
            acc = [acc[t] + jnp.where(own_tiles[q] == t, value, 0.0) for t in range(4)]
        return jnp.concatenate(acc, 1)

    def z2(l, way, t):
        return remote(
            ring.at[l, way, t], got2.at[l, way, t], sz2.at[4 * l + 2 * way + t // 2, t % 2],
            rz2.at[4 * l + 2 * way + t // 2, t % 2], onward(way),
        )

    for t in range(4):
        for l, way in chains:
            if t == 0 and way == 0:
                for q in (1, 2, 3):
                    remote(
                        send2.at[l, slot_of(q)], mid2.at[l, slot_of(q)], s2.at[l, q], r2.at[l, q], at_slot(q)
                    ).wait_recv()
            if t >= hops(l, way):
                continue
            to_z = on(way, hops(l, way) - t)
            mine_in = [placed(l, to_z, part) for part in range(2)]
            if t:
                z2(l, way, t - 1).wait_recv()
                mine_in = [mine_in[part] + got2[l, way, t - 1, part].astype(F32) for part in range(2)]
            for part in range(2):
                ring[l, way, t, part] = mine_in[part].astype(BF16)
            z2(l, way, t).start()

    def z3(l, way, t):
        block = recv3.at[l, on(1 - way, t)]
        return remote(
            block, block, sz3.at[4 * l + 2 * way + t // 2, t % 2], rz3.at[4 * l + 2 * way + t // 2, t % 2], onward(way)
        )

    def z3_in(l, way, t):
        block = recv3.at[l, on(1 - way, t + 1)]
        return remote(
            block, block, sz3.at[4 * l + 2 * way + t // 2, t % 2], rz3.at[4 * l + 2 * way + t // 2, t % 2], onward(way)
        )

    load_w.wait()
    for l in range(PAIR):
        g = [placed(l, z, part) for part in range(2)]
        for way in (1 - l, l):
            last = hops(l, way) - 1
            z2(l, way, last).wait_recv()
            g = [g[part] + got2[l, way, last, part].astype(F32) for part in range(2)]
        v = dot(jnp.concatenate(g, 0).astype(BF16), f_tab[...])
        weight = w_buf[:, l, :]
        h_real = weight * (v[:BLOCK, :XM] + v[BLOCK:, XM:])
        h_imag = weight * (v[BLOCK:, :XM] - v[:BLOCK, XM:])
        v = dot(jnp.concatenate([h_real, h_imag], 0).astype(BF16), f_tab[...])
        recv3[l, z, 0] = (v[:BLOCK, :XM] - v[BLOCK:, XM:]).astype(BF16)
        recv3[l, z, 1] = (v[BLOCK:, :XM] + v[:BLOCK, XM:]).astype(BF16)
        for way in range(2):
            z3(l, way, 0).start()
        spectra[:, l, 0, :] = h_real
        spectra[:, l, 1, :] = h_imag
    store_s = pltpu.make_async_copy(spectra, spectra_hbm, out_sem.at[1])
    store_s.start()

    tiles = [tiles_of(lax.rem(low + q // 2, 2) * 16 + z * 2 + lax.rem(core + q % 2, 2)) for q in range(4)]

    def windows(l, from_z):
        for part in range(2):
            whole = recv3[l, from_z, part].astype(F32)
            cut = [whole[:, M * t : M * t + M] for t in range(4)]
            for q in range(4):
                one = jnp.where(tiles[q] == 1, cut[1], cut[0])
                two = jnp.where(tiles[q] == 3, cut[3], cut[2])
                one = jnp.where(tiles[q] < 2, one, two).astype(BF16)
                if q:
                    win3[l, q, from_z, part] = one
                else:
                    rows3[l, slot, from_z, part] = one

    for l in range(PAIR):
        windows(l, z)
    for t in range(3):
        for l, way in chains:
            z3_in(l, way, t).wait_recv()
            if t + 1 < hops(l, way):
                z3(l, way, t + 1).start()
        for l, way in chains:
            windows(l, on(1 - way, t + 1))
    for l in range(PAIR):
        z3_in(l, l, 3).wait_recv()
        windows(l, on(1 - l, 4))
        for q in (3, 2, 1):
            remote(win3.at[l, q], rows3.at[l, slot], s3.at[l, q], r3.at[l, q], at_slot(q)).start()

    e_here = e_there = None
    for l in range(PAIR):
        for q in (1, 2, 3):
            remote(win3.at[l, q], rows3.at[l, slot_of(q)], s3.at[l, q], r3.at[l, q], at_slot(q)).wait_recv()
        rows = jnp.concatenate([rows3[l, :, :, 0].reshape(XM, M), rows3[l, :, :, 1].reshape(XM, M)], 1)
        u = dot_t(rows, r_tab[...])
        recv4[l, x] = jnp.concatenate([u[:M, :M] - u[M:, M:], u[M:, :M] + u[:M, M:]], 1).astype(BF16)
        for d in (2, 1, 3):
            remote(recv4.at[l, x], recv4.at[l, x], s4.at[l, d], r4.at[l, d], at_x(d)).start()

    for l in range(PAIR):
        for d in (0, 1, 3, 2):
            from_x = lax.rem(x + 4 - d, 4)
            if d:
                remote(recv4.at[l, from_x], recv4.at[l, from_x], s4.at[l, d], r4.at[l, d], at_x(d)).wait_recv()
            v = recv4[l, from_x]
            v = jnp.concatenate([v, jnp.concatenate([v[:, M:], -v[:, :M]], 1)], 0)
            there = dot(v, p_tab[1 - hi, 2 * from_x + l])
            here = dot(v, p_tab[hi, 2 * from_x + l])
            e_there = there if e_there is None else e_there + there
            e_here = here if e_here is None else e_here + here
    send5[...] = e_there.astype(BF16)
    swap_e = remote(send5, recv5, s5, r5, across)
    swap_e.start()
    for l in range(PAIR):
        for d in range(1, 4):
            remote(send1.at[l, d], recv1.at[l, d], s1.at[l, d], r1.at[l, d], at_x(d)).wait_send()
            remote(recv4.at[l, x], recv4.at[l, x], s4.at[l, d], r4.at[l, d], at_x(d)).wait_send()
            remote(send2.at[l, slot_of(d)], mid2.at[l, slot], s2.at[l, d], r2.at[l, d], at_slot(d)).wait_send()
            remote(win3.at[l, d], rows3.at[l, slot], s3.at[l, d], r3.at[l, d], at_slot(d)).wait_send()
        for way in range(2):
            for t in range(hops(l, way)):
                z2(l, way, t).wait_send()
                z3(l, way, t).wait_send()
    store_q.wait()
    store_s.wait()
    swap_e.wait_recv()
    e = (e_here + recv5[...].astype(F32)).astype(BF16)
    et_out[...] = dot(perm[...], e).astype(BF16)
    store_e = pltpu.make_async_copy(et_out, et_hbm, out_sem.at[2])
    store_e.start()
    swap_e.wait_send()
    store_e.wait()


def correction(et_hbm, q_hbm, spectra_in, out, spectra, et, q, buf, load_sem, sems, sem):
    copy = pltpu.make_async_copy(spectra_in, spectra, sem)
    copy.start()
    parts = buf.shape[0]
    width = buf.shape[3]
    load = pltpu.make_async_copy(et_hbm, et, load_sem.at[parts])
    load.start()
    tables = [
        pltpu.make_async_copy(q_hbm.at[:, pl.ds(width * i, width)], q.at[i], load_sem.at[i]) for i in range(parts)
    ]
    for table in tables:
        table.start()
    gain = 2.0 * math.sqrt(YF / M)
    load.wait()
    real = et[...]
    imag = jnp.concatenate([real[M:], -real[:M]], 0)
    moves = []
    for i in range(parts):
        tables[i].wait()
        buf[i, 0] = (dot_t(real, q[i]) * gain).astype(BF16)
        buf[i, 1] = (dot_t(imag, q[i]) * gain).astype(BF16)
        move = pltpu.make_async_copy(buf.at[i], out.at[0, :, :, pl.ds(width * i, width)], sems.at[i])
        move.start()
        moves.append(move)
    for move in moves:
        move.wait()
    copy.wait()


def shards(facets, weights, facet_offsets, subgrid_offsets, column):
    hbm = pl.BlockSpec(memory_space=pl.ANY)
    dma = pltpu.SemaphoreType.DMA
    pair_of = lambda *shape: pltpu.VMEM((PAIR, *shape), BF16)
    et, q, spectra = pl.pallas_call(
        round_trip,
        out_shape=(
            jax.ShapeDtypeStruct((2 * M, ROWS), BF16),
            jax.ShapeDtypeStruct((2 * M, YF), BF16),
            jax.ShapeDtypeStruct((BLOCK, PAIR, 2, XM), F32),
        ),
        in_specs=[hbm] * 5,
        out_specs=(hbm, hbm, hbm),
        scratch_shapes=[
            pltpu.VMEM((2 * M, ROWS), BF16),
            pltpu.VMEM((2 * M, YF), BF16),
            pltpu.VMEM((BLOCK, PAIR, 2, XM), F32),
            pltpu.SMEM((2, FACETS), jnp.int32),
            pltpu.SMEM((SUBS,), jnp.int32),
            pltpu.SMEM((1,), jnp.int32),
            pltpu.VMEM((2, ROWS, YF), BF16),
            pltpu.VMEM((BLOCK, PAIR, XM), F32),
            pltpu.VMEM((8, YF), F32),
            pltpu.VMEM((8, YF), F32),
            pltpu.VMEM((16, YF), F32),
            pltpu.VMEM((16, YF), F32),
            pltpu.VMEM((2, 8, 2 * M, ROWS), BF16),
            pltpu.VMEM((XM, 2 * XM), BF16),
            pltpu.VMEM((XM, 2 * M), BF16),
            pltpu.VMEM((2 * M, 2 * M), BF16),
            pltpu.VMEM((2, ROWS, 2 * M), BF16),
            pair_of(4, M, 2 * M),
            pair_of(4, M, 2 * M),
            pair_of(4, 8, 2, BLOCK, M),
            pair_of(4, 8, 2, BLOCK, M),
            pair_of(2, 4, 2, BLOCK, XM),
            pair_of(2, 4, 2, BLOCK, XM),
            pair_of(8, 2, BLOCK, XM),
            pair_of(4, 8, 2, BLOCK, M),
            pair_of(4, 8, 2, BLOCK, M),
            pair_of(4, M, 2 * M),
            pltpu.VMEM((2 * M, ROWS), BF16),
            pltpu.VMEM((2 * M, ROWS), BF16),
            dma((3,)), dma((3,)), dma, dma,
            dma, dma,
            dma((PAIR, 4)), dma((PAIR, 4)),
            dma((PAIR, 4)), dma((PAIR, 4)),
            dma((8, 2)), dma((8, 2)),
            dma((8, 2)), dma((8, 2)),
            dma((PAIR, 4)), dma((PAIR, 4)),
            dma((PAIR, 4)), dma((PAIR, 4)),
            dma, dma,
        ],
        compiler_params=pltpu.CompilerParams(
            collective_id=0, has_side_effects=True, vmem_limit_bytes=VMEM_MIB * 2**20
        ),
        cost_estimate=pl.CostEstimate(flops=3 * 10**9, bytes_accessed=4 * 10**6, transcendentals=0),
        name="round_trip",
    )(facets, weights, facet_offsets.T, subgrid_offsets, column)
    parts = 4
    update, spectra = pl.pallas_call(
        correction,
        out_shape=(
            jax.ShapeDtypeStruct((1, 2, ROWS, YF), BF16),
            jax.ShapeDtypeStruct((BLOCK, PAIR, 2, XM), F32),
        ),
        in_specs=[hbm] * 3,
        out_specs=(hbm, hbm),
        scratch_shapes=[
            pltpu.VMEM((2 * M, ROWS), BF16),
            pltpu.VMEM((parts, 2 * M, YF // parts), BF16),
            pltpu.VMEM((parts, 2, ROWS, YF // parts), BF16),
            dma((parts + 1,)),
            dma((parts,)),
            dma,
        ],
        compiler_params=pltpu.CompilerParams(vmem_limit_bytes=VMEM_MIB * 2**20),
        cost_estimate=pl.CostEstimate(flops=10**9, bytes_accessed=3 * 10**6, transcendentals=0),
        name="correction",
    )(et, q, spectra)
    return update, spectra


def solution(mesh):
    return jax.shard_map(
        shards,
        mesh=mesh,
        in_specs=(
            P("facet", None, ("half", "sub"), None),
            P("facet", ("half", "sub"), None),
            P(),
            P(),
            P(),
        ),
        out_specs=(
            P("facet", None, ("half", "sub"), None),
            P("facet", ("half", "sub"), None, None),
        ),
        check_vma=False,
    )
```

```python
import functools
import math

import jax
import jax.numpy as jnp
from jax import lax
from jax.experimental import pallas as pl
from jax.experimental.pallas import tpu as pltpu
from jax.sharding import PartitionSpec as P

YF = 2048
M = 128
XM = 512
SUBS = 16
FACETS = 32
PAIR = 2
ROWS = 256
BLOCK = 16
VMEM_MIB = 52
MESH = pl.DeviceIdType.MESH
F32 = jnp.float32
BF16 = jnp.bfloat16


def cis(turn, n):
    quarter = n // 4
    q = lax.shift_right_logical(turn + n // 8, quarter.bit_length() - 1)
    x = (turn - q * quarter).astype(F32) * (2.0 * math.pi / n)
    z = x * x
    s = x + x * z * (-1.6666654611e-1 + z * (8.3321608736e-3 - 1.9515295891e-4 * z))
    c = 1.0 - 0.5 * z + z * z * (4.166664568298827e-2 + z * (-1.388731625493765e-3 + 2.443315711809948e-5 * z))
    swap = (q & 1) == 1
    cosine = jnp.where(swap, s, c)
    sine = jnp.where(swap, c, s)
    cosine = jnp.where(((q + 1) & 2) != 0, -cosine, cosine)
    sine = jnp.where((q & 2) != 0, -sine, sine)
    return cosine, sine


def iota(shape, dim):
    return lax.broadcasted_iota(jnp.int32, shape, dim)


def taper(pos):
    _, s = cis(2 * pos + 1, 4 * YF)
    return s * s * (1.0 / math.sqrt(YF))


def dot(a, b):
    return jnp.dot(a, b, preferred_element_type=F32)


def dot_t(a, b):
    return lax.dot_general(a, b, (((0,), (0,)), ((), ())), preferred_element_type=F32)


def remote(src, dst, send, recv, to):
    return pltpu.make_async_remote_copy(
        src_ref=src, dst_ref=dst, send_sem=send, recv_sem=recv, device_id=to, device_id_type=MESH
    )


def round_trip(
    facets, weights, foff_in, soff_in, col_in,
    et_out, q_out, spectra,
    foff, soff, col, x_buf, w_buf, hi_c, hi_s, lo_c, lo_s, p_tab, f_tab, r_tab, perm,
    a_buf, p_own, send1, recv1, send2, recv2, send3, recv3, recv4, send5, recv5,
    small_sem, x_sem, w_sem, sa, ra, s1, r1, s2, r2, s3, r3, s4, r4, s5, r5,
):
    mine = lax.axis_index("facet")
    x = lax.axis_index("half")
    hi = lax.axis_index("sub")
    core = lax.rem(mine, 2)
    z = lax.rem(mine // 2, 8)
    low = mine // 16

    def at_x(d):
        return {"half": lax.rem(x + d, 4)}

    def peer(i, j):
        dz = 4 + ((i + 1) // 2) * (1 - 2 * lax.rem(i, 2))
        return lax.rem(low + 1 - j // 2, 2) * 16 + lax.rem(z + dz, 8) * 2 + lax.rem(core + 1 - j % 2, 2)

    across = {"sub": 1 - hi}

    smalls = [
        pltpu.make_async_copy(src, dst, small_sem.at[i])
        for i, (src, dst) in enumerate([(col_in, col), (foff_in, foff), (soff_in, soff)])
    ]
    for copy in smalls:
        copy.start()
    load = pltpu.make_async_copy(facets.at[0], x_buf, x_sem)
    load.start()
    load_w = pltpu.make_async_copy(weights, w_buf, w_sem)
    load_w.start()

    barrier = pltpu.get_barrier_semaphore()
    friends = [across] + [at_x(d) for d in (1, 2, 3)]
    for to in friends:
        pl.semaphore_signal(barrier, inc=1, device_id=to, device_id_type=MESH)

    @pl.loop(1, FACETS)
    def _(i):
        to = {"facet": lax.rem(mine + i, FACETS)}
        pl.semaphore_signal(barrier, inc=1, device_id=to, device_id_type=MESH)

    y = iota((8, YF), 1)
    c, s = cis(iota((16, YF), 0) * iota((16, YF), 1) & (YF - 1), YF)
    w = taper(iota((1, YF), 1))
    lo_c[...] = c * w
    lo_s[...] = s * w
    for copy in smalls:
        copy.wait()
    c, s = cis(((col[0] + 16 * iota((8, YF), 0)) & (YF - 1)) * y & (YF - 1), YF)
    hi_c[...] = c
    hi_s[...] = s

    @pl.loop(0, 8)
    def _(a):
        hc, hs = hi_c[pl.ds(a, 1), :], hi_s[pl.ds(a, 1), :]
        lc, ls = lo_c[...], lo_s[...]
        at = pl.multiple_of(a * 16, 16)
        q_out[pl.ds(at, 16), :] = (hc * lc - hs * ls).astype(BF16)
        q_out[pl.ds(at + M, 16), :] = (-(hs * lc + hc * ls)).astype(BF16)

    turn = foff[1, mine] & (M - 1)
    k, c = iota((2 * M, 2 * M), 0), iota((2 * M, 2 * M), 1)
    same = ((k & (M - 1)) == ((c - turn) & (M - 1))) & ((k < M) == (c < M))
    perm[...] = jnp.where(same, 1.0, 0.0).astype(BF16)

    load.wait()
    q = q_out[...]
    over = (((1,), (1,)), ((), ()))
    from_real = lax.dot_general(x_buf[0], q, over, preferred_element_type=F32)
    from_imag = lax.dot_general(x_buf[1], q, over, preferred_element_type=F32)
    a_both = jnp.concatenate(
        [from_real[:, :M] - from_imag[:, M:], from_real[:, M:] + from_imag[:, :M]], 1
    ).astype(BF16)
    a_buf[hi] = dot(a_both, perm[...]).astype(BF16)

    pl.semaphore_wait(barrier, len(friends) + FACETS - 1)
    swap_a = remote(a_buf.at[hi], a_buf.at[hi], sa, ra, across)
    swap_a.start()

    first = x * (2 * ROWS)
    pos = first + iota((16, 2 * ROWS), 1)
    c, s = cis(iota((16, 2 * ROWS), 0) * pos & (YF - 1), YF)
    w = taper(first + iota((1, 2 * ROWS), 1))
    lc, ls = c * w, s * w

    @pl.loop(0, 2 * 4)
    def _(u):
        freq = (soff[4 * (u // 2) + 2 * hi + lax.rem(u, 2)] + 16 * iota((8, 2 * ROWS), 0)) & (YF - 1)
        hc, hs = cis(freq * (first + iota((8, 2 * ROWS), 1)) & (YF - 1), YF)
        for a in range(8):
            c, s = hc[a : a + 1], hs[a : a + 1]
            real = (c * lc - s * ls).astype(BF16)
            imag = (-(s * lc + c * ls)).astype(BF16)
            for b in range(2):
                p_tab[b, u, 16 * a : 16 * a + 16, :] = real[:, ROWS * b : ROWS * b + ROWS]
                p_tab[b, u, M + 16 * a : M + 16 * a + 16, :] = imag[:, ROWS * b : ROWS * b + ROWS]

    @pl.loop(0, 2 * 4)
    def _(u):
        p_own[u] = dot(p_tab[hi, u], a_buf[hi])

    def partial(l, to_x):
        u = 2 * to_x + l
        v = p_own[u] + dot(p_tab[1 - hi, u], a_buf[1 - hi])
        return jnp.concatenate([v[:M, :M] - v[M:, M:], v[:M, M:] + v[M:, :M]], 1).astype(BF16)

    swap_a.wait()
    for l in range(PAIR):
        for d in (2, 1, 3):
            send1[l, d] = partial(l, lax.rem(x + d, 4))
            remote(send1.at[l, d], recv1.at[l, d], s1.at[l, d], r1.at[l, d], at_x(d)).start()
        recv1[l, 0] = partial(l, x)

    scale = 1.0 / math.sqrt(XM)
    place = (foff[0, mine] + iota((16, M), 1)) & (XM - 1)
    lc, ls = cis(iota((16, M), 0) * place & (XM - 1), XM)
    lc, ls = lc * scale, ls * scale
    place = (foff[0, mine] + iota((32, M), 1)) & (XM - 1)
    hc, hs = cis(16 * iota((32, M), 0) * place & (XM - 1), XM)
    for a in range(32):
        c, s = hc[a : a + 1], hs[a : a + 1]
        r_tab[16 * a : 16 * a + 16, :M] = (c * lc - s * ls).astype(BF16)
        r_tab[16 * a : 16 * a + 16, M:] = (s * lc + c * ls).astype(BF16)

    c, s = cis(16 * iota((32, XM), 0) * iota((32, XM), 1) & (XM - 1), XM)
    lc, ls = cis(iota((16, XM), 0) * iota((16, XM), 1) & (XM - 1), XM)
    lc, ls = lc * scale, ls * scale
    for a in range(32):
        hc, hs = c[a : a + 1], s[a : a + 1]
        f_tab[16 * a : 16 * a + 16, :XM] = (hc * lc - hs * ls).astype(BF16)
        f_tab[16 * a : 16 * a + 16, XM:] = (hs * lc + hc * ls).astype(BF16)

    def bulk(send, recv, l, ssem, rsem):
        some = pl.ds(0, FACETS - 1)
        return remote(send.at[l, some], recv.at[l, some], ssem.at[l], rsem.at[l], {"facet": peer(0, 0)})

    def to_all(action):
        @pl.loop(0, 7)
        def _(i):
            for j in range(4):
                action(peer(i, j))

        for j in range(3):
            action(peer(7, j))

    for l in range(PAIR):
        total = recv1[l, 0].astype(F32)
        for d in (1, 3, 2):
            remote(send1.at[l, d], recv1.at[l, d], s1.at[l, d], r1.at[l, d], at_x(d)).wait_recv()
            total = total + recv1[l, d].astype(F32)
        total = total.astype(BF16)
        cr, ci = total[:, :M], total[:, M:]
        both = jnp.concatenate([jnp.concatenate([cr, ci], 1), jnp.concatenate([ci, -cr], 1)], 0)
        kk = dot(r_tab[...], both).astype(BF16)
        send2[l, :, 0] = kk[:, :M].reshape(FACETS, BLOCK, M)
        send2[l, :, 1] = kk[:, M:].reshape(FACETS, BLOCK, M)
        to_all(lambda f: remote(send2.at[l, f], recv2.at[l, mine], s2.at[l], r2.at[l], {"facet": f}).start())
        recv2[l, mine] = send2[l, mine]

    lane = iota((BLOCK, M), 1)

    def tiles_of(f):
        o = foff[1, f]
        return (lax.shift_right_logical(o, 7) + jnp.where(lane < (o & (M - 1)), 1, 0)) & 3

    load_w.wait()
    for l in range(PAIR):
        bulk(send2, recv2, l, s2, r2).wait_recv()

        def gather(i, acc):
            for f in (2 * i, 2 * i + 1):
                tile = tiles_of(f)
                got = [recv2[l, f, part].astype(F32) for part in range(2)]
                acc = tuple(
                    acc[4 * part + t] + jnp.where(tile == t, got[part], 0.0) for part in range(2) for t in range(4)
                )
            return acc

        acc = lax.fori_loop(0, FACETS // 2, gather, (jnp.zeros((BLOCK, M), F32),) * 8)
        g = jnp.concatenate([jnp.concatenate(acc[:4], 1), jnp.concatenate(acc[4:], 1)], 0).astype(BF16)
        v = dot(g, f_tab[...])
        weight = w_buf[:, l, :]
        h_real = weight * (v[:BLOCK, :XM] + v[BLOCK:, XM:])
        h_imag = weight * (v[BLOCK:, :XM] - v[:BLOCK, XM:])
        v = dot(jnp.concatenate([h_real, h_imag], 0).astype(BF16), f_tab[...])
        space = [v[:BLOCK, :XM] - v[BLOCK:, XM:], v[BLOCK:, :XM] + v[:BLOCK, XM:]]

        def window(f):
            tile = tiles_of(f)
            for part in range(2):
                cut = [space[part][:, M * t : M * t + M] for t in range(4)]
                one = jnp.where(tile == 1, cut[1], cut[0])
                two = jnp.where(tile == 3, cut[3], cut[2])
                send3[l, f, part] = jnp.where(tile < 2, one, two).astype(BF16)

        def window_out(f):
            window(f)
            remote(send3.at[l, f], recv3.at[l, mine], s3.at[l], r3.at[l], {"facet": f}).start()

        to_all(window_out)
        window(mine)
        recv3[l, mine] = send3[l, mine]
        spectra[:, l, 0, :] = h_real
        spectra[:, l, 1, :] = h_imag

    for l in range(PAIR):
        bulk(send3, recv3, l, s3, r3).wait_recv()
        rows = jnp.concatenate([recv3[l, :, 0].reshape(XM, M), recv3[l, :, 1].reshape(XM, M)], 1)
        u = dot_t(rows, r_tab[...])
        recv4[l, x] = jnp.concatenate([u[:M, :M] - u[M:, M:], u[M:, :M] + u[:M, M:]], 1).astype(BF16)
        for d in (2, 1, 3):
            remote(recv4.at[l, x], recv4.at[l, x], s4.at[l, d], r4.at[l, d], at_x(d)).start()

    def spread(l, d, block):
        from_x = lax.rem(x + 4 - d, 4)
        v = recv4[l, from_x]
        v = jnp.concatenate([v, jnp.concatenate([v[:, M:], -v[:, :M]], 1)], 0)
        return dot(v, p_tab[block, 2 * from_x + l])

    e_there = e_here = None
    for l in range(PAIR):
        for d in (0, 1, 3, 2):
            from_x = lax.rem(x + 4 - d, 4)
            if d:
                remote(recv4.at[l, from_x], recv4.at[l, from_x], s4.at[l, d], r4.at[l, d], at_x(d)).wait_recv()
            there = spread(l, d, 1 - hi)
            e_there = there if e_there is None else e_there + there
            if l == 0:
                here = spread(l, d, hi)
                e_here = here if e_here is None else e_here + here
    send5[...] = e_there.astype(BF16)
    swap_e = remote(send5, recv5, s5, r5, across)
    swap_e.start()
    for d in (0, 1, 3, 2):
        e_here = e_here + spread(1, d, hi)
    for l in range(PAIR):
        bulk(send2, recv2, l, s2, r2).wait_send()
        bulk(send3, recv3, l, s3, r3).wait_send()
        for d in range(1, 4):
            remote(send1.at[l, d], recv1.at[l, d], s1.at[l, d], r1.at[l, d], at_x(d)).wait_send()
            remote(recv4.at[l, x], recv4.at[l, x], s4.at[l, d], r4.at[l, d], at_x(d)).wait_send()
    swap_e.wait_recv()
    e = (e_here + recv5[...].astype(F32)).astype(BF16)
    et_out[...] = dot(perm[...], e).astype(BF16)
    swap_e.wait_send()


def correction(et, q, spectra_in, out, spectra, buf, sems, sem):
    copy = pltpu.make_async_copy(spectra_in, spectra, sem)
    copy.start()
    gain = 2.0 * math.sqrt(YF / M)
    real = et[...]
    imag = jnp.concatenate([real[M:], -real[:M]], 0)
    parts = buf.shape[0]
    width = buf.shape[3]
    moves = []
    for i in range(parts):
        table = q[:, width * i : width * i + width]
        buf[i, 0] = (dot_t(real, table) * gain).astype(BF16)
        buf[i, 1] = (dot_t(imag, table) * gain).astype(BF16)
        move = pltpu.make_async_copy(buf.at[i], out.at[0, :, :, pl.ds(width * i, width)], sems.at[i])
        move.start()
        moves.append(move)
    for move in moves:
        move.wait()
    copy.wait()


def shards(facets, weights, facet_offsets, subgrid_offsets, column):
    hbm = pl.BlockSpec(memory_space=pltpu.HBM)
    anywhere = pl.BlockSpec(memory_space=pl.ANY)
    vmem = pl.BlockSpec(memory_space=pltpu.VMEM)
    dma = pltpu.SemaphoreType.DMA
    pair_of = lambda *shape: pltpu.VMEM((PAIR, *shape), BF16)
    et, q, spectra = pl.pallas_call(
        round_trip,
        out_shape=(
            jax.ShapeDtypeStruct((2 * M, ROWS), BF16),
            jax.ShapeDtypeStruct((2 * M, YF), BF16),
            jax.ShapeDtypeStruct((BLOCK, PAIR, 2, XM), F32),
        ),
        in_specs=[hbm] * 5,
        out_specs=(vmem, vmem, vmem),
        scratch_shapes=[
            pltpu.SMEM((2, FACETS), jnp.int32),
            pltpu.SMEM((SUBS,), jnp.int32),
            pltpu.SMEM((1,), jnp.int32),
            pltpu.VMEM((2, ROWS, YF), BF16),
            pltpu.VMEM((BLOCK, PAIR, XM), F32),
            pltpu.VMEM((8, YF), F32),
            pltpu.VMEM((8, YF), F32),
            pltpu.VMEM((16, YF), F32),
            pltpu.VMEM((16, YF), F32),
            pltpu.VMEM((2, 8, 2 * M, ROWS), BF16),
            pltpu.VMEM((XM, 2 * XM), BF16),
            pltpu.VMEM((XM, 2 * M), BF16),
            pltpu.VMEM((2 * M, 2 * M), BF16),
            pltpu.VMEM((2, ROWS, 2 * M), BF16),
            pltpu.VMEM((8, 2 * M, 2 * M), F32),
            pair_of(4, M, 2 * M),
            pair_of(4, M, 2 * M),
            pair_of(FACETS, 2, BLOCK, M),
            pair_of(FACETS, 2, BLOCK, M),
            pair_of(FACETS, 2, BLOCK, M),
            pair_of(FACETS, 2, BLOCK, M),
            pair_of(4, M, 2 * M),
            pltpu.VMEM((2 * M, ROWS), BF16),
            pltpu.VMEM((2 * M, ROWS), BF16),
            dma((3,)), dma, dma,
            dma, dma,
            dma((PAIR, 4)), dma((PAIR, 4)),
            dma((PAIR,)), dma((PAIR,)),
            dma((PAIR,)), dma((PAIR,)),
            dma((PAIR, 4)), dma((PAIR, 4)),
            dma, dma,
        ],
        compiler_params=pltpu.CompilerParams(
            collective_id=0, has_side_effects=True, vmem_limit_bytes=VMEM_MIB * 2**20
        ),
        cost_estimate=pl.CostEstimate(flops=3 * 10**9, bytes_accessed=4 * 10**6, transcendentals=0),
        name="round_trip",
    )(facets, weights, facet_offsets.T, subgrid_offsets, column)
    parts = 4
    update, spectra = pl.pallas_call(
        correction,
        out_shape=(
            jax.ShapeDtypeStruct((1, 2, ROWS, YF), BF16),
            jax.ShapeDtypeStruct((BLOCK, PAIR, 2, XM), F32),
        ),
        in_specs=[vmem, vmem, anywhere],
        out_specs=(hbm, hbm),
        scratch_shapes=[
            pltpu.VMEM((parts, 2, ROWS, YF // parts), BF16),
            dma((parts,)),
            dma,
        ],
        compiler_params=pltpu.CompilerParams(vmem_limit_bytes=24 * 2**20),
        cost_estimate=pl.CostEstimate(flops=10**9, bytes_accessed=3 * 10**6, transcendentals=0),
        name="correction",
    )(et, q, spectra)
    return update, spectra


def solution(mesh):
    return jax.shard_map(
        shards,
        mesh=mesh,
        in_specs=(
            P("facet", None, ("half", "sub"), None),
            P("facet", ("half", "sub"), None),
            P(),
            P(),
            P(),
        ),
        out_specs=(
            P("facet", None, ("half", "sub"), None),
            P("facet", ("half", "sub"), None, None),
        ),
        check_vma=False,
    )
```

```python
import functools
import math

import jax
import jax.numpy as jnp
from jax import lax
from jax.experimental import pallas as pl
from jax.experimental.pallas import tpu as pltpu
from jax.sharding import PartitionSpec as P

YF = 2048
M = 128
XM = 512
SUBS = 16
FACETS = 32
PAIR = 2
ROWS = 256
BLOCK = 16
PIECES = 4
VMEM_MIB = 60
MESH = pl.DeviceIdType.MESH
F32 = jnp.float32
BF16 = jnp.bfloat16


def cis(turn, n):
    quarter = n // 4
    q = lax.shift_right_logical(turn + n // 8, quarter.bit_length() - 1)
    x = (turn - q * quarter).astype(F32) * (2.0 * math.pi / n)
    z = x * x
    s = x + x * z * (-1.6666654611e-1 + z * (8.3321608736e-3 - 1.9515295891e-4 * z))
    c = 1.0 - 0.5 * z + z * z * (4.166664568298827e-2 + z * (-1.388731625493765e-3 + 2.443315711809948e-5 * z))
    swap = (q & 1) == 1
    cosine = jnp.where(swap, s, c)
    sine = jnp.where(swap, c, s)
    cosine = jnp.where(((q + 1) & 2) != 0, -cosine, cosine)
    sine = jnp.where((q & 2) != 0, -sine, sine)
    return cosine, sine


def iota(shape, dim):
    return lax.broadcasted_iota(jnp.int32, shape, dim)


def taper(pos):
    _, s = cis(2 * pos + 1, 4 * YF)
    return s * s * (1.0 / math.sqrt(YF))


def dot(a, b):
    return jnp.dot(a, b, preferred_element_type=F32)


def dot_t(a, b):
    return lax.dot_general(a, b, (((0,), (0,)), ((), ())), preferred_element_type=F32)


def remote(src, dst, send, recv, to):
    return pltpu.make_async_remote_copy(
        src_ref=src, dst_ref=dst, send_sem=send, recv_sem=recv, device_id=to, device_id_type=MESH
    )


def round_trip(
    facets, weights, foff_in, soff_in, col_in,
    et_hbm, q_hbm, spectra_hbm,
    et_out, q_out, q_turned, spectra, foff, soff, col, x_buf, w_buf, hi_c, hi_s, lo_c, lo_s, p_tab, p_wide, f_tab, r_tab, perm,
    a_low, a_high, kept, send1, recv1, send2, recv2, send3, recv3, recv4, recv4y, send5, recv5,
    out_sem, small_sem, x_sem, w_sem, sa, ra, s1, r1, s2, r2, s3, r3, s4, r4, s5, r5,
):
    mine = lax.axis_index("facet")
    x = lax.axis_index("half")
    hi = lax.axis_index("sub")
    core = lax.rem(mine, 2)
    z = lax.rem(mine // 2, 8)
    low = mine // 16

    def at_x(d):
        return {"half": lax.rem(x + d, 4)}

    def peer(i, j):
        dz = 4 + ((i + 1) // 2) * (1 - 2 * lax.rem(i, 2))
        return lax.rem(low + 1 - j // 2, 2) * 16 + lax.rem(z + dz, 8) * 2 + lax.rem(core + 1 - j % 2, 2)

    across = {"sub": 1 - hi}

    smalls = [
        pltpu.make_async_copy(src, dst, small_sem.at[i])
        for i, (src, dst) in enumerate([(col_in, col), (foff_in, foff), (soff_in, soff)])
    ]
    for copy in smalls:
        copy.start()
    width = YF // PIECES
    loads = [
        pltpu.make_async_copy(facets.at[0, :, :, pl.ds(width * i, width)], x_buf.at[i], x_sem.at[i])
        for i in range(PIECES)
    ]
    for load in loads:
        load.start()
    load_w = pltpu.make_async_copy(weights, w_buf, w_sem)
    load_w.start()

    barrier = pltpu.get_barrier_semaphore()
    friends = [across] + [at_x(d) for d in (1, 2, 3)]
    for to in friends:
        pl.semaphore_signal(barrier, inc=1, device_id=to, device_id_type=MESH)

    @pl.loop(1, FACETS)
    def _(i):
        to = {"facet": lax.rem(mine + i, FACETS)}
        pl.semaphore_signal(barrier, inc=1, device_id=to, device_id_type=MESH)

    y = iota((8, YF), 1)
    c, s = cis(iota((16, YF), 0) * iota((16, YF), 1) & (YF - 1), YF)
    w = taper(iota((1, YF), 1))
    lo_c[...] = c * w
    lo_s[...] = s * w
    for copy in smalls:
        copy.wait()
    c, s = cis(((col[0] + 16 * iota((8, YF), 0)) & (YF - 1)) * y & (YF - 1), YF)
    hi_c[...] = c
    hi_s[...] = s

    @pl.loop(0, 8)
    def _(a):
        hc, hs = hi_c[pl.ds(a, 1), :], hi_s[pl.ds(a, 1), :]
        lc, ls = lo_c[...], lo_s[...]
        at = pl.multiple_of(a * 16, 16)
        q_out[pl.ds(at, 16), :] = (hc * lc - hs * ls).astype(BF16)
        q_out[pl.ds(at + M, 16), :] = (-(hs * lc + hc * ls)).astype(BF16)

    turn = foff[1, mine] & (M - 1)
    r, c = iota((2 * M, 2 * M), 0), iota((2 * M, 2 * M), 1)
    k = lax.shift_right_logical(c, 7) * 64 + (c & 63)
    same = ((r & (M - 1)) == ((k - turn) & (M - 1))) & (lax.shift_right_logical(r, 7) == (lax.shift_right_logical(c, 6) & 1))
    perm[...] = jnp.where(same, 1.0, 0.0).astype(BF16)

    over = (((1,), (1,)), ((), ()))
    from_real = from_imag = None
    for i, load in enumerate(loads):
        load.wait()
        q = q_out[:, width * i : width * i + width]
        real = lax.dot_general(x_buf[i, 0], q, over, preferred_element_type=F32)
        imag = lax.dot_general(x_buf[i, 1], q, over, preferred_element_type=F32)
        from_real = real if i == 0 else from_real + real
        from_imag = imag if i == 0 else from_imag + imag
    a_both = jnp.concatenate(
        [from_real[:, :M] - from_imag[:, M:], from_real[:, M:] + from_imag[:, :M]], 1
    ).astype(BF16)
    a_both = dot(a_both, perm[...]).astype(BF16)
    a_low[hi] = a_both[:, :M]
    a_high[x] = a_both[:, M:]

    pl.semaphore_wait(barrier, len(friends) + FACETS - 1)

    def swap_a(d):
        if d:
            return remote(a_high.at[x], a_high.at[x], sa.at[d], ra.at[d], at_x(d))
        return remote(a_low.at[hi], a_low.at[hi], sa.at[0], ra.at[0], across)

    for d in (2, 0, 1, 3):
        swap_a(d).start()

    first = x * (2 * ROWS)
    pos = first + iota((16, 2 * ROWS), 1)
    c, s = cis(iota((16, 2 * ROWS), 0) * pos & (YF - 1), YF)
    w = taper(first + iota((1, 2 * ROWS), 1))
    lc, ls = c * w, s * w

    @pl.loop(0, 2 * 4)
    def _(u):
        freq = (soff[4 * (u // 2) + 2 * hi + lax.rem(u, 2)] + 16 * iota((8, 2 * ROWS), 0)) & (YF - 1)
        hc, hs = cis(freq * (first + iota((8, 2 * ROWS), 1)) & (YF - 1), YF)
        for a in range(8):
            c, s = hc[a : a + 1], hs[a : a + 1]
            real = (c * lc - s * ls).astype(BF16)
            imag = (-(s * lc + c * ls)).astype(BF16)
            for b in range(2):
                p_tab[b, u, 16 * a : 16 * a + 16, :] = real[:, ROWS * b : ROWS * b + ROWS]
                p_tab[b, u, M + 16 * a : M + 16 * a + 16, :] = imag[:, ROWS * b : ROWS * b + ROWS]

    for b in range(4):
        first_b = (2 * b + hi) * ROWS
        c, s = cis(iota((16, ROWS), 0) * (first_b + iota((16, ROWS), 1)) & (YF - 1), YF)
        w = taper(first_b + iota((1, ROWS), 1))
        lc_b, ls_b = c * w, s * w

        @pl.loop(0, 4)
        def _(u):
            freq = (soff[4 * x + u] + 16 * iota((8, ROWS), 0)) & (YF - 1)
            hc, hs = cis(freq * (first_b + iota((8, ROWS), 1)) & (YF - 1), YF)
            for a in range(8):
                c, s = hc[a : a + 1], hs[a : a + 1]
                p_wide[b, u, 16 * a : 16 * a + 16, :] = (c * lc_b - s * ls_b).astype(BF16)
                p_wide[b, u, M + 16 * a : M + 16 * a + 16, :] = (-(s * lc_b + c * ls_b)).astype(BF16)

    left = iota((M, M), 1) < 64

    def complex_sum(v):
        turned = pltpu.roll(v[M:], 64, 1)
        return v[:M] + jnp.where(left, -turned, turned)

    for u in range(8):
        kept[u] = dot(p_tab[hi, u], a_low[hi])
    for u in range(4):
        kept[8 + u] = dot(p_wide[x, u], a_high[x])

    def partial_low(l, to_x):
        u = 2 * to_x + l
        return complex_sum(kept[u] + dot(p_tab[1 - hi, u], a_low[1 - hi]))

    def partial_high(l, to_hi):
        u = 2 * to_hi + l
        v = kept[8 + u]
        for d in (1, 3, 2):
            v = v + dot(p_wide[lax.rem(x + 4 - d, 4), u], a_high[lax.rem(x + 4 - d, 4)])
        return complex_sum(v)

    def sum1(l, d):
        return remote(send1.at[l, d], recv1.at[l, d], s1.at[l, d], r1.at[l, d], at_x(d) if d else across)

    for d in (0, 1, 3, 2):
        if d:
            block = a_high.at[lax.rem(x + 4 - d, 4)]
            remote(block, block, sa.at[d], ra.at[d], at_x(d)).wait_recv()
        else:
            remote(a_low.at[1 - hi], a_low.at[1 - hi], sa.at[0], ra.at[0], across).wait_recv()
            for d_low in (2, 1, 3):
                send1[0, d_low] = partial_low(0, lax.rem(x + d_low, 4)).astype(BF16)
                sum1(0, d_low).start()
    own = []
    for l in range(PAIR):
        send1[l, 0] = partial_high(l, 1 - hi).astype(BF16)
        sum1(l, 0).start()
        if l:
            for d in (2, 1, 3):
                send1[l, d] = partial_low(l, lax.rem(x + d, 4)).astype(BF16)
                sum1(l, d).start()
    for l in range(PAIR):
        own.append((partial_low(l, x), partial_high(l, hi)))

    q_turned[...] = dot_t(perm[...], q_out[...]).astype(BF16)
    store_q = pltpu.make_async_copy(q_turned, q_hbm, out_sem.at[0])
    store_q.start()

    scale = 1.0 / math.sqrt(XM)
    place = (foff[0, mine] + iota((16, M), 1)) & (XM - 1)
    lc, ls = cis(iota((16, M), 0) * place & (XM - 1), XM)
    lc, ls = lc * scale, ls * scale
    place = (foff[0, mine] + iota((32, M), 1)) & (XM - 1)
    hc, hs = cis(16 * iota((32, M), 0) * place & (XM - 1), XM)
    for a in range(32):
        c, s = hc[a : a + 1], hs[a : a + 1]
        r_tab[16 * a : 16 * a + 16, :M] = (c * lc - s * ls).astype(BF16)
        r_tab[16 * a : 16 * a + 16, M:] = (s * lc + c * ls).astype(BF16)

    c, s = cis(16 * iota((32, XM), 0) * iota((32, XM), 1) & (XM - 1), XM)
    lc, ls = cis(iota((16, XM), 0) * iota((16, XM), 1) & (XM - 1), XM)
    lc, ls = lc * scale, ls * scale
    for a in range(32):
        hc, hs = c[a : a + 1], s[a : a + 1]
        f_tab[16 * a : 16 * a + 16, :XM] = (hc * lc - hs * ls).astype(BF16)
        f_tab[16 * a : 16 * a + 16, XM:] = (hs * lc + hc * ls).astype(BF16)

    def bulk(send, recv, l, ssem, rsem):
        some = pl.ds(0, FACETS - 1)
        return remote(send.at[l, some], recv.at[l, some], ssem.at[l], rsem.at[l], {"facet": peer(0, 0)})

    def to_all(action):
        @pl.loop(0, 7)
        def _(i):
            for j in range(4):
                action(peer(i, j))

        for j in range(3):
            action(peer(7, j))

    for l in range(PAIR):
        low_k, high_k = own[l]
        for d in (0, 1, 3, 2):
            sum1(l, d).wait_recv()
            if d:
                low_k = low_k + recv1[l, d].astype(F32)
            else:
                high_k = high_k + recv1[l, d].astype(F32)
        cr = jnp.where(left, low_k, pltpu.roll(high_k, 64, 1)).astype(BF16)
        ci = jnp.where(left, pltpu.roll(low_k, 64, 1), high_k).astype(BF16)
        both = jnp.concatenate([jnp.concatenate([cr, ci], 1), jnp.concatenate([ci, -cr], 1)], 0)
        kk = dot(r_tab[...], both).astype(BF16)
        send2[l, :, 0] = kk[:, :M].reshape(FACETS, BLOCK, M)
        send2[l, :, 1] = kk[:, M:].reshape(FACETS, BLOCK, M)
        to_all(lambda f: remote(send2.at[l, f], recv2.at[l, mine], s2.at[l], r2.at[l], {"facet": f}).start())
        recv2[l, mine] = send2[l, mine]

    lane = iota((BLOCK, M), 1)

    def tiles_of(f):
        o = foff[1, f]
        return (lax.shift_right_logical(o, 7) + jnp.where(lane < (o & (M - 1)), 1, 0)) & 3

    load_w.wait()
    for l in range(PAIR):
        bulk(send2, recv2, l, s2, r2).wait_recv()

        def gather(i, acc):
            for f in (2 * i, 2 * i + 1):
                tile = tiles_of(f)
                got = [recv2[l, f, part].astype(F32) for part in range(2)]
                acc = tuple(
                    acc[4 * part + t] + jnp.where(tile == t, got[part], 0.0) for part in range(2) for t in range(4)
                )
            return acc

        acc = lax.fori_loop(0, FACETS // 2, gather, (jnp.zeros((BLOCK, M), F32),) * 8)
        g = jnp.concatenate([jnp.concatenate(acc[:4], 1), jnp.concatenate(acc[4:], 1)], 0).astype(BF16)
        v = dot(g, f_tab[...])
        weight = w_buf[:, l, :]
        h_real = weight * (v[:BLOCK, :XM] + v[BLOCK:, XM:])
        h_imag = weight * (v[BLOCK:, :XM] - v[:BLOCK, XM:])
        v = dot(jnp.concatenate([h_real, h_imag], 0).astype(BF16), f_tab[...])
        space = [v[:BLOCK, :XM] - v[BLOCK:, XM:], v[BLOCK:, :XM] + v[:BLOCK, XM:]]

        def window(f):
            tile = tiles_of(f)
            for part in range(2):
                cut = [space[part][:, M * t : M * t + M] for t in range(4)]
                one = jnp.where(tile == 1, cut[1], cut[0])
                two = jnp.where(tile == 3, cut[3], cut[2])
                send3[l, f, part] = jnp.where(tile < 2, one, two).astype(BF16)

        def window_out(f):
            window(f)
            remote(send3.at[l, f], recv3.at[l, mine], s3.at[l], r3.at[l], {"facet": f}).start()

        to_all(window_out)
        window(mine)
        recv3[l, mine] = send3[l, mine]
        spectra[:, l, 0, :] = h_real
        spectra[:, l, 1, :] = h_imag
    store_s = pltpu.make_async_copy(spectra, spectra_hbm, out_sem.at[1])
    store_s.start()

    def send4(l, d):
        if d:
            return remote(recv4.at[l, x], recv4.at[l, x], s4.at[l, d], r4.at[l, d], at_x(d))
        return remote(recv4y.at[l, hi], recv4y.at[l, hi], s4.at[l, 0], r4.at[l, 0], across)

    def swap_e(d):
        return remote(send5.at[d], recv5.at[d], s5.at[d], r5.at[d], at_x(d) if d else across)

    for l in range(PAIR):
        bulk(send3, recv3, l, s3, r3).wait_recv()
        rows = jnp.concatenate([recv3[l, :, 0].reshape(XM, M), recv3[l, :, 1].reshape(XM, M)], 1)
        u = dot_t(rows, r_tab[...])
        d_both = jnp.concatenate([u[:M, :M] - u[M:, M:], u[M:, :M] + u[:M, M:]], 1).astype(BF16)
        recv4[l, x] = d_both[:64]
        recv4y[l, hi] = d_both[64:]
        for d in (2, 0, 1, 3):
            send4(l, d).start()

    def twice(v):
        return jnp.concatenate([v, jnp.concatenate([v[:, M:], -v[:, :M]], 1)], 0)

    def add(total, term):
        return term if total is None else total + term

    low_e, high_e = [None, None], [None] * 4
    for l in range(PAIR):
        for d in (0, 1, 3, 2):
            from_x = lax.rem(x + 4 - d, 4)
            if d:
                block = recv4.at[l, from_x]
                remote(block, block, s4.at[l, d], r4.at[l, d], at_x(d)).wait_recv()
            else:
                block = recv4y.at[l, 1 - hi]
                remote(block, block, s4.at[l, d], r4.at[l, d], across).wait_recv()
                for near_hi in (hi, 1 - hi):
                    v = twice(recv4y[l, near_hi])
                    for e in (2, 1, 3) if l else (2, 1, 3, 0):
                        high_e[e] = add(high_e[e], dot(v, p_wide[lax.rem(x + e, 4), 2 * near_hi + l]))
                if l:
                    for e in (2, 1, 3):
                        send5[e] = high_e[e].astype(BF16)
                        swap_e(e).start()
            v = twice(recv4[l, from_x])
            low_e[1] = add(low_e[1], dot(v, p_tab[1 - hi, 2 * from_x + l]))
            if l == 0:
                low_e[0] = add(low_e[0], dot(v, p_tab[hi, 2 * from_x]))
    send5[0] = low_e[1].astype(BF16)
    swap_e(0).start()
    for d in range(4):
        from_x = lax.rem(x + 4 - d, 4)
        low_e[0] = low_e[0] + dot(twice(recv4[1, from_x]), p_tab[hi, 2 * from_x + 1])
    for near_hi in range(2):
        high_e[0] = high_e[0] + dot(twice(recv4y[1, near_hi]), p_wide[x, 2 * near_hi + 1])
    for l in range(PAIR):
        bulk(send2, recv2, l, s2, r2).wait_send()
        bulk(send3, recv3, l, s3, r3).wait_send()
        for d in range(4):
            sum1(l, d).wait_send()
            send4(l, d).wait_send()
    for d in range(4):
        swap_a(d).wait_send()
    store_q.wait()
    store_s.wait()
    low_k, high_k = low_e[0], high_e[0]
    for d in (1, 3, 2, 0):
        swap_e(d).wait_recv()
        if d:
            high_k = high_k + recv5[d].astype(F32)
        else:
            low_k = low_k + recv5[d].astype(F32)
    et_out[...] = jnp.concatenate([low_k, high_k], 0).astype(BF16)
    store_e = pltpu.make_async_copy(et_out, et_hbm, out_sem.at[2])
    store_e.start()
    for d in range(4):
        swap_e(d).wait_send()
    store_e.wait()


def correction(et_hbm, q_hbm, spectra_in, out, spectra_out, et, q, spectra, buf, load_sem, store_sem):
    parts = buf.shape[0]
    width = buf.shape[3]
    load = pltpu.make_async_copy(et_hbm, et, load_sem.at[parts])
    load.start()
    tables = [
        pltpu.make_async_copy(q_hbm.at[:, pl.ds(width * i, width)], q.at[i], load_sem.at[i]) for i in range(parts)
    ]
    for table in tables:
        table.start()
    load_s = pltpu.make_async_copy(spectra_in, spectra, load_sem.at[parts + 1])
    load_s.start()
    gain = 2.0 * math.sqrt(YF / M)
    load.wait()
    real = et[...]
    imag = jnp.concatenate([real[64:128], -real[:64], real[192:], -real[128:192]], 0)
    moves = []
    for i in range(parts):
        tables[i].wait()
        buf[i, 0] = (dot_t(real, q[i]) * gain).astype(BF16)
        buf[i, 1] = (dot_t(imag, q[i]) * gain).astype(BF16)
        moves.append(pltpu.make_async_copy(buf.at[i], out.at[0, :, :, pl.ds(width * i, width)], store_sem.at[i]))
        moves[-1].start()
        if i == 0:
            load_s.wait()
            moves.append(pltpu.make_async_copy(spectra, spectra_out, store_sem.at[parts]))
            moves[-1].start()
    for move in moves:
        move.wait()


def shards(facets, weights, facet_offsets, subgrid_offsets, column):
    hbm = pl.BlockSpec(memory_space=pltpu.HBM)
    dma = pltpu.SemaphoreType.DMA
    pair_of = lambda *shape: pltpu.VMEM((PAIR, *shape), BF16)
    et, q, spectra = pl.pallas_call(
        round_trip,
        out_shape=(
            jax.ShapeDtypeStruct((2 * M, ROWS), BF16),
            jax.ShapeDtypeStruct((2 * M, YF), BF16),
            jax.ShapeDtypeStruct((BLOCK, PAIR, 2, XM), F32),
        ),
        in_specs=[hbm] * 5,
        out_specs=(hbm, hbm, hbm),
        scratch_shapes=[
            pltpu.VMEM((2 * M, ROWS), BF16),
            pltpu.VMEM((2 * M, YF), BF16),
            pltpu.VMEM((2 * M, YF), BF16),
            pltpu.VMEM((BLOCK, PAIR, 2, XM), F32),
            pltpu.SMEM((2, FACETS), jnp.int32),
            pltpu.SMEM((SUBS,), jnp.int32),
            pltpu.SMEM((1,), jnp.int32),
            pltpu.VMEM((PIECES, 2, ROWS, YF // PIECES), BF16),
            pltpu.VMEM((BLOCK, PAIR, XM), F32),
            pltpu.VMEM((8, YF), F32),
            pltpu.VMEM((8, YF), F32),
            pltpu.VMEM((16, YF), F32),
            pltpu.VMEM((16, YF), F32),
            pltpu.VMEM((2, 8, 2 * M, ROWS), BF16),
            pltpu.VMEM((4, 4, 2 * M, ROWS), BF16),
            pltpu.VMEM((XM, 2 * XM), BF16),
            pltpu.VMEM((XM, 2 * M), BF16),
            pltpu.VMEM((2 * M, 2 * M), BF16),
            pltpu.VMEM((2, ROWS, M), BF16),
            pltpu.VMEM((4, ROWS, M), BF16),
            pltpu.VMEM((12, 2 * M, M), F32),
            pair_of(4, M, M),
            pair_of(4, M, M),
            pair_of(FACETS, 2, BLOCK, M),
            pair_of(FACETS, 2, BLOCK, M),
            pair_of(FACETS, 2, BLOCK, M),
            pair_of(FACETS, 2, BLOCK, M),
            pair_of(4, 64, 2 * M),
            pair_of(2, 64, 2 * M),
            pltpu.VMEM((4, M, ROWS), BF16),
            pltpu.VMEM((4, M, ROWS), BF16),
            dma((3,)), dma((3,)), dma((PIECES,)), dma,
            dma((4,)), dma((4,)),
            dma((PAIR, 4)), dma((PAIR, 4)),
            dma((PAIR,)), dma((PAIR,)),
            dma((PAIR,)), dma((PAIR,)),
            dma((PAIR, 4)), dma((PAIR, 4)),
            dma((4,)), dma((4,)),
        ],
        compiler_params=pltpu.CompilerParams(
            collective_id=0, has_side_effects=True, vmem_limit_bytes=VMEM_MIB * 2**20
        ),
        cost_estimate=pl.CostEstimate(flops=3 * 10**9, bytes_accessed=4 * 10**6, transcendentals=0),
        name="round_trip",
    )(facets, weights, facet_offsets.T, subgrid_offsets, column)
    parts = 4
    update, spectra = pl.pallas_call(
        correction,
        out_shape=(
            jax.ShapeDtypeStruct((1, 2, ROWS, YF), BF16),
            jax.ShapeDtypeStruct((BLOCK, PAIR, 2, XM), F32),
        ),
        in_specs=[hbm] * 3,
        out_specs=(hbm, hbm),
        scratch_shapes=[
            pltpu.VMEM((2 * M, ROWS), BF16),
            pltpu.VMEM((parts, 2 * M, YF // parts), BF16),
            pltpu.VMEM((BLOCK, PAIR, 2, XM), F32),
            pltpu.VMEM((parts, 2, ROWS, YF // parts), BF16),
            dma((parts + 2,)),
            dma((parts + 1,)),
        ],
        compiler_params=pltpu.CompilerParams(vmem_limit_bytes=VMEM_MIB * 2**20),
        cost_estimate=pl.CostEstimate(flops=10**9, bytes_accessed=3 * 10**6, transcendentals=0),
        name="correction",
    )(et, q, spectra)
    return update, spectra


def solution(mesh):
    return jax.shard_map(
        shards,
        mesh=mesh,
        in_specs=(
            P("facet", None, ("half", "sub"), None),
            P("facet", ("half", "sub"), None),
            P(),
            P(),
            P(),
        ),
        out_specs=(
            P("facet", None, ("half", "sub"), None),
            P("facet", ("half", "sub"), None, None),
        ),
        check_vma=False,
    )
```

```python
import functools
import math

import jax
import jax.numpy as jnp
from jax import lax
from jax.experimental import pallas as pl
from jax.experimental.pallas import tpu as pltpu
from jax.sharding import PartitionSpec as P

YF = 2048
M = 128
XM = 512
SUBS = 16
FACETS = 32
PAIR = 2
ROWS = 256
BLOCK = 16
PIECES = 4
VMEM_MIB = 52
MESH = pl.DeviceIdType.MESH
F32 = jnp.float32
BF16 = jnp.bfloat16


def cis(turn, n):
    quarter = n // 4
    q = lax.shift_right_logical(turn + n // 8, quarter.bit_length() - 1)
    x = (turn - q * quarter).astype(F32) * (2.0 * math.pi / n)
    z = x * x
    s = x + x * z * (-1.6666654611e-1 + z * (8.3321608736e-3 - 1.9515295891e-4 * z))
    c = 1.0 - 0.5 * z + z * z * (4.166664568298827e-2 + z * (-1.388731625493765e-3 + 2.443315711809948e-5 * z))
    swap = (q & 1) == 1
    cosine = jnp.where(swap, s, c)
    sine = jnp.where(swap, c, s)
    cosine = jnp.where(((q + 1) & 2) != 0, -cosine, cosine)
    sine = jnp.where((q & 2) != 0, -sine, sine)
    return cosine, sine


def iota(shape, dim):
    return lax.broadcasted_iota(jnp.int32, shape, dim)


def taper(pos):
    _, s = cis(2 * pos + 1, 4 * YF)
    return s * s * (1.0 / math.sqrt(YF))


def dot(a, b):
    return jnp.dot(a, b, preferred_element_type=F32)


def dot_t(a, b):
    return lax.dot_general(a, b, (((0,), (0,)), ((), ())), preferred_element_type=F32)


def remote(src, dst, send, recv, to):
    return pltpu.make_async_remote_copy(
        src_ref=src, dst_ref=dst, send_sem=send, recv_sem=recv, device_id=to, device_id_type=MESH
    )


def round_trip(
    facets, weights, offsets_in,
    et_out, q_turned, spectra,
    q_out, offsets, x_buf, w_buf, hi_c, hi_s, lo_c, lo_s, p_tab, p_wide, f_tab, r_tab, perm,
    a_low, a_high, kept, send1, recv1, send2, recv2, send3, recv3, recv4, recv4y, send5, recv5,
    small_sem, x_sem, w_sem, sa, ra, s1, r1, s2, r2, s3, r3, s4, r4, s5, r5,
):
    mine = lax.axis_index("facet")
    x = lax.axis_index("half")
    hi = lax.axis_index("sub")
    core = lax.rem(mine, 2)
    z = lax.rem(mine // 2, 8)
    low = mine // 16

    def at_x(d):
        return {"half": lax.rem(x + d, 4)}

    def peer(i, dy, dc):
        dz = 4 + ((i + 1) // 2) * (1 - 2 * lax.rem(i, 2))
        return lax.rem(low + dy, 2) * 16 + lax.rem(z + dz, 8) * 2 + lax.rem(core + dc, 2)

    across = {"sub": 1 - hi}

    load_o = pltpu.make_async_copy(offsets_in, offsets, small_sem)
    load_o.start()
    width = YF // PIECES
    loads = [
        pltpu.make_async_copy(facets.at[0, :, :, pl.ds(width * i, width)], x_buf.at[i], x_sem.at[i])
        for i in range(PIECES)
    ]
    for load in loads:
        load.start()
    load_w = pltpu.make_async_copy(weights, w_buf, w_sem)
    load_w.start()

    barrier = pltpu.get_barrier_semaphore()
    friends = [across] + [at_x(d) for d in (1, 2, 3)]
    for to in friends:
        pl.semaphore_signal(barrier, inc=1, device_id=to, device_id_type=MESH)

    @pl.loop(1, FACETS)
    def _(i):
        to = {"facet": lax.rem(mine + i, FACETS)}
        pl.semaphore_signal(barrier, inc=1, device_id=to, device_id_type=MESH)

    y = iota((8, YF), 1)
    c, s = cis(iota((16, YF), 0) * iota((16, YF), 1) & (YF - 1), YF)
    w = taper(iota((1, YF), 1))
    lo_c[...] = c * w
    lo_s[...] = s * w
    load_o.wait()
    c, s = cis(((offsets[3, 0] + 16 * iota((8, YF), 0)) & (YF - 1)) * y & (YF - 1), YF)
    hi_c[...] = c
    hi_s[...] = s

    @pl.loop(0, 8)
    def _(a):
        hc, hs = hi_c[pl.ds(a, 1), :], hi_s[pl.ds(a, 1), :]
        lc, ls = lo_c[...], lo_s[...]
        at = pl.multiple_of(a * 16, 16)
        q_out[pl.ds(at, 16), :] = (hc * lc - hs * ls).astype(BF16)
        q_out[pl.ds(at + M, 16), :] = (-(hs * lc + hc * ls)).astype(BF16)

    turn = offsets[1, mine] & (M - 1)
    r, c = iota((2 * M, 2 * M), 0), iota((2 * M, 2 * M), 1)
    k = lax.shift_right_logical(c, 7) * 64 + (c & 63)
    same = ((r & (M - 1)) == ((k - turn) & (M - 1))) & (lax.shift_right_logical(r, 7) == (lax.shift_right_logical(c, 6) & 1))
    perm[...] = jnp.where(same, 1.0, 0.0).astype(BF16)

    over = (((1,), (1,)), ((), ()))
    from_real = from_imag = None
    for i, load in enumerate(loads):
        load.wait()
        q = q_out[:, width * i : width * i + width]
        real = lax.dot_general(x_buf[i, 0], q, over, preferred_element_type=F32)
        imag = lax.dot_general(x_buf[i, 1], q, over, preferred_element_type=F32)
        from_real = real if i == 0 else from_real + real
        from_imag = imag if i == 0 else from_imag + imag
    a_both = jnp.concatenate(
        [from_real[:, :M] - from_imag[:, M:], from_real[:, M:] + from_imag[:, :M]], 1
    ).astype(BF16)
    a_both = dot(a_both, perm[...]).astype(BF16)
    a_low[hi] = a_both[:, :M]
    a_high[x] = a_both[:, M:]

    pl.semaphore_wait(barrier, len(friends) + FACETS - 1)

    def swap_a(d):
        if d:
            return remote(a_high.at[x], a_high.at[x], sa.at[d], ra.at[d], at_x(d))
        return remote(a_low.at[hi], a_low.at[hi], sa.at[0], ra.at[0], across)

    for d in (2, 0, 1, 3):
        swap_a(d).start()

    first = x * (2 * ROWS)
    pos = first + iota((16, 2 * ROWS), 1)
    c, s = cis(iota((16, 2 * ROWS), 0) * pos & (YF - 1), YF)
    w = taper(first + iota((1, 2 * ROWS), 1))
    lc, ls = c * w, s * w

    @pl.loop(0, 2 * 4)
    def _(u):
        freq = (offsets[2, 4 * (u // 2) + 2 * hi + lax.rem(u, 2)] + 16 * iota((8, 2 * ROWS), 0)) & (YF - 1)
        hc, hs = cis(freq * (first + iota((8, 2 * ROWS), 1)) & (YF - 1), YF)
        for a in range(8):
            c, s = hc[a : a + 1], hs[a : a + 1]
            real = (c * lc - s * ls).astype(BF16)
            imag = (-(s * lc + c * ls)).astype(BF16)
            for b in range(2):
                p_tab[b, u, 16 * a : 16 * a + 16, :] = real[:, ROWS * b : ROWS * b + ROWS]
                p_tab[b, u, M + 16 * a : M + 16 * a + 16, :] = imag[:, ROWS * b : ROWS * b + ROWS]

    for b in range(4):
        first_b = (2 * b + hi) * ROWS
        c, s = cis(iota((16, ROWS), 0) * (first_b + iota((16, ROWS), 1)) & (YF - 1), YF)
        w = taper(first_b + iota((1, ROWS), 1))
        lc_b, ls_b = c * w, s * w

        @pl.loop(0, 4)
        def _(u):
            freq = (offsets[2, 4 * x + u] + 16 * iota((8, ROWS), 0)) & (YF - 1)
            hc, hs = cis(freq * (first_b + iota((8, ROWS), 1)) & (YF - 1), YF)
            for a in range(8):
                c, s = hc[a : a + 1], hs[a : a + 1]
                p_wide[b, u, 16 * a : 16 * a + 16, :] = (c * lc_b - s * ls_b).astype(BF16)
                p_wide[b, u, M + 16 * a : M + 16 * a + 16, :] = (-(s * lc_b + c * ls_b)).astype(BF16)

    left = iota((M, M), 1) < 64

    def complex_sum(v):
        turned = pltpu.roll(v[M:], 64, 1)
        return v[:M] + jnp.where(left, -turned, turned)

    for u in range(8):
        kept[u] = dot(p_tab[hi, u], a_low[hi])
    for u in range(4):
        kept[8 + u] = dot(p_wide[x, u], a_high[x])

    def partial_low(l, to_x):
        u = 2 * to_x + l
        return complex_sum(kept[u] + dot(p_tab[1 - hi, u], a_low[1 - hi]))

    def partial_high(l, to_hi):
        u = 2 * to_hi + l
        v = kept[8 + u]
        for d in (1, 3, 2):
            v = v + dot(p_wide[lax.rem(x + 4 - d, 4), u], a_high[lax.rem(x + 4 - d, 4)])
        return complex_sum(v)

    def sum1(l, d):
        return remote(send1.at[l, d], recv1.at[l, d], s1.at[l, d], r1.at[l, d], at_x(d) if d else across)

    for d in (0, 1, 3, 2):
        if d:
            block = a_high.at[lax.rem(x + 4 - d, 4)]
            remote(block, block, sa.at[d], ra.at[d], at_x(d)).wait_recv()
        else:
            remote(a_low.at[1 - hi], a_low.at[1 - hi], sa.at[0], ra.at[0], across).wait_recv()
            for d_low in (2, 1, 3):
                send1[0, d_low] = partial_low(0, lax.rem(x + d_low, 4)).astype(BF16)
                sum1(0, d_low).start()
    own = []
    for l in range(PAIR):
        send1[l, 0] = partial_high(l, 1 - hi).astype(BF16)
        sum1(l, 0).start()
        if l:
            for d in (2, 1, 3):
                send1[l, d] = partial_low(l, lax.rem(x + d, 4)).astype(BF16)
                sum1(l, d).start()
    for l in range(PAIR):
        own.append((partial_low(l, x), partial_high(l, hi)))

    q_turned[...] = dot_t(perm[...], q_out[...]).astype(BF16)

    scale = 1.0 / math.sqrt(XM)
    place = (offsets[0, mine] + iota((16, M), 1)) & (XM - 1)
    lc, ls = cis(iota((16, M), 0) * place & (XM - 1), XM)
    lc, ls = lc * scale, ls * scale
    place = (offsets[0, mine] + iota((32, M), 1)) & (XM - 1)
    hc, hs = cis(16 * iota((32, M), 0) * place & (XM - 1), XM)
    for a in range(32):
        c, s = hc[a : a + 1], hs[a : a + 1]
        r_tab[16 * a : 16 * a + 16, :M] = (c * lc - s * ls).astype(BF16)
        r_tab[16 * a : 16 * a + 16, M:] = (s * lc + c * ls).astype(BF16)

    c, s = cis(16 * iota((32, XM), 0) * iota((32, XM), 1) & (XM - 1), XM)
    lc, ls = cis(iota((16, XM), 0) * iota((16, XM), 1) & (XM - 1), XM)
    lc, ls = lc * scale, ls * scale
    for a in range(32):
        hc, hs = c[a : a + 1], s[a : a + 1]
        f_tab[16 * a : 16 * a + 16, :XM] = (hc * lc - hs * ls).astype(BF16)
        f_tab[16 * a : 16 * a + 16, XM:] = (hs * lc + hc * ls).astype(BF16)

    def bulk(send, recv, l, ssem, rsem):
        some = pl.ds(0, FACETS - 1)
        return remote(send.at[l, some], recv.at[l, some], ssem.at[l], rsem.at[l], {"facet": peer(0, 0, 0)})

    def to_all(action):
        for dc in (1, 0):

            @pl.loop(0, 7 + dc)
            def _(i):
                for dy in (1, 0):
                    action(peer(i, dy, dc))

        action(peer(7, 1, 0))

    for l in range(PAIR):
        low_k, high_k = own[l]
        for d in (0, 1, 3, 2):
            sum1(l, d).wait_recv()
            if d:
                low_k = low_k + recv1[l, d].astype(F32)
            else:
                high_k = high_k + recv1[l, d].astype(F32)
        cr = jnp.where(left, low_k, pltpu.roll(high_k, 64, 1)).astype(BF16)
        ci = jnp.where(left, pltpu.roll(low_k, 64, 1), high_k).astype(BF16)
        both = jnp.concatenate([jnp.concatenate([cr, ci], 1), jnp.concatenate([ci, -cr], 1)], 0)
        kk = dot(r_tab[...], both).astype(BF16)
        send2[l, :, 0] = kk[:, :M].reshape(FACETS, BLOCK, M)
        send2[l, :, 1] = kk[:, M:].reshape(FACETS, BLOCK, M)
        to_all(lambda f: remote(send2.at[l, f], recv2.at[l, mine], s2.at[l], r2.at[l], {"facet": f}).start())
        recv2[l, mine] = send2[l, mine]

    lane = iota((BLOCK, M), 1)

    def tiles_of(f):
        o = offsets[1, f]
        return (lax.shift_right_logical(o, 7) + jnp.where(lane < (o & (M - 1)), 1, 0)) & 3

    load_w.wait()
    for l in range(PAIR):
        bulk(send2, recv2, l, s2, r2).wait_recv()

        def gather(i, acc):
            for f in (2 * i, 2 * i + 1):
                tile = tiles_of(f)
                got = [recv2[l, f, part].astype(F32) for part in range(2)]
                acc = tuple(
                    acc[4 * part + t] + jnp.where(tile == t, got[part], 0.0) for part in range(2) for t in range(4)
                )
            return acc

        acc = lax.fori_loop(0, FACETS // 2, gather, (jnp.zeros((BLOCK, M), F32),) * 8)
        g = jnp.concatenate([jnp.concatenate(acc[:4], 1), jnp.concatenate(acc[4:], 1)], 0).astype(BF16)
        v = dot(g, f_tab[...])
        weight = w_buf[:, l, :]
        h_real = weight * (v[:BLOCK, :XM] + v[BLOCK:, XM:])
        h_imag = weight * (v[BLOCK:, :XM] - v[:BLOCK, XM:])
        v = dot(jnp.concatenate([h_real, h_imag], 0).astype(BF16), f_tab[...])
        space = [v[:BLOCK, :XM] - v[BLOCK:, XM:], v[BLOCK:, :XM] + v[:BLOCK, XM:]]

        def window(f):
            tile = tiles_of(f)
            for part in range(2):
                cut = [space[part][:, M * t : M * t + M] for t in range(4)]
                one = jnp.where(tile == 1, cut[1], cut[0])
                two = jnp.where(tile == 3, cut[3], cut[2])
                send3[l, f, part] = jnp.where(tile < 2, one, two).astype(BF16)

        def window_out(f):
            window(f)
            remote(send3.at[l, f], recv3.at[l, mine], s3.at[l], r3.at[l], {"facet": f}).start()

        to_all(window_out)
        window(mine)
        recv3[l, mine] = send3[l, mine]
        spectra[:, l, 0, :] = h_real
        spectra[:, l, 1, :] = h_imag

    def send4(l, d):
        if d:
            return remote(recv4.at[l, x], recv4.at[l, x], s4.at[l, d], r4.at[l, d], at_x(d))
        return remote(recv4y.at[l, hi], recv4y.at[l, hi], s4.at[l, 0], r4.at[l, 0], across)

    def swap_e(d):
        return remote(send5.at[d], recv5.at[d], s5.at[d], r5.at[d], at_x(d) if d else across)

    for l in range(PAIR):
        bulk(send3, recv3, l, s3, r3).wait_recv()
        rows = jnp.concatenate([recv3[l, :, 0].reshape(XM, M), recv3[l, :, 1].reshape(XM, M)], 1)
        u = dot_t(rows, r_tab[...])
        d_both = jnp.concatenate([u[:M, :M] - u[M:, M:], u[M:, :M] + u[:M, M:]], 1).astype(BF16)
        recv4[l, x] = d_both[:64]
        recv4y[l, hi] = d_both[64:]
        for d in (2, 0, 1, 3):
            send4(l, d).start()

    def twice(v):
        return jnp.concatenate([v, jnp.concatenate([v[:, M:], -v[:, :M]], 1)], 0)

    def add(total, term):
        return term if total is None else total + term

    low_e, high_e = [None, None], [None] * 4
    for l in range(PAIR):
        for d in (0, 1, 3, 2):
            from_x = lax.rem(x + 4 - d, 4)
            if d:
                block = recv4.at[l, from_x]
                remote(block, block, s4.at[l, d], r4.at[l, d], at_x(d)).wait_recv()
            else:
                block = recv4y.at[l, 1 - hi]
                remote(block, block, s4.at[l, d], r4.at[l, d], across).wait_recv()
                for near_hi in (hi, 1 - hi):
                    v = twice(recv4y[l, near_hi])
                    for e in (2, 1, 3) if l else (2, 1, 3, 0):
                        high_e[e] = add(high_e[e], dot(v, p_wide[lax.rem(x + e, 4), 2 * near_hi + l]))
                if l:
                    for e in (2, 1, 3):
                        send5[e] = high_e[e].astype(BF16)
                        swap_e(e).start()
            v = twice(recv4[l, from_x])
            low_e[1] = add(low_e[1], dot(v, p_tab[1 - hi, 2 * from_x + l]))
            if l == 0:
                low_e[0] = add(low_e[0], dot(v, p_tab[hi, 2 * from_x]))
    send5[0] = low_e[1].astype(BF16)
    swap_e(0).start()
    for d in range(4):
        from_x = lax.rem(x + 4 - d, 4)
        low_e[0] = low_e[0] + dot(twice(recv4[1, from_x]), p_tab[hi, 2 * from_x + 1])
    for near_hi in range(2):
        high_e[0] = high_e[0] + dot(twice(recv4y[1, near_hi]), p_wide[x, 2 * near_hi + 1])
    for l in range(PAIR):
        bulk(send2, recv2, l, s2, r2).wait_send()
        bulk(send3, recv3, l, s3, r3).wait_send()
        for d in range(4):
            sum1(l, d).wait_send()
            send4(l, d).wait_send()
    for d in range(4):
        swap_a(d).wait_send()
    low_k, high_k = low_e[0], high_e[0]
    for d in (1, 3, 2, 0):
        swap_e(d).wait_recv()
        if d:
            high_k = high_k + recv5[d].astype(F32)
        else:
            low_k = low_k + recv5[d].astype(F32)
    et_out[...] = jnp.concatenate([low_k, high_k], 0).astype(BF16)
    for d in range(4):
        swap_e(d).wait_send()


def correction(et, q, spectra_in, out, spectra_out, buf, sems):
    parts = buf.shape[0]
    width = buf.shape[3]
    moves = [pltpu.make_async_copy(spectra_in, spectra_out, sems.at[parts])]
    moves[0].start()
    gain = 2.0 * math.sqrt(YF / M)
    real = et[...]
    imag = jnp.concatenate([real[64:128], -real[:64], real[192:], -real[128:192]], 0)
    for i in range(parts):
        table = q[:, width * i : width * i + width]
        buf[i, 0] = (dot_t(real, table) * gain).astype(BF16)
        buf[i, 1] = (dot_t(imag, table) * gain).astype(BF16)
        moves.append(pltpu.make_async_copy(buf.at[i], out.at[0, :, :, pl.ds(width * i, width)], sems.at[i]))
        moves[-1].start()
    for move in moves:
        move.wait()


def shards(facets, weights, facet_offsets, subgrid_offsets, column):
    hbm = pl.BlockSpec(memory_space=pltpu.HBM)
    anywhere = pl.BlockSpec(memory_space=pl.ANY)
    vmem = pl.BlockSpec(memory_space=pltpu.VMEM)
    dma = pltpu.SemaphoreType.DMA
    pair_of = lambda *shape: pltpu.VMEM((PAIR, *shape), BF16)
    zero = jnp.int32(0)
    offsets = (
        lax.pad(facet_offsets.T, zero, [(0, 2, 0), (0, 0, 0)])
        + lax.pad(subgrid_offsets[None], zero, [(2, 1, 0), (0, FACETS - SUBS, 0)])
        + lax.pad(column[None], zero, [(3, 0, 0), (0, FACETS - 1, 0)])
    )
    et, q, spectra = pl.pallas_call(
        round_trip,
        out_shape=(
            jax.ShapeDtypeStruct((2 * M, ROWS), BF16),
            jax.ShapeDtypeStruct((2 * M, YF), BF16),
            jax.ShapeDtypeStruct((BLOCK, PAIR, 2, XM), F32),
        ),
        in_specs=[hbm] * 3,
        out_specs=(vmem, vmem, vmem),
        scratch_shapes=[
            pltpu.VMEM((2 * M, YF), BF16),
            pltpu.SMEM((4, FACETS), jnp.int32),
            pltpu.VMEM((PIECES, 2, ROWS, YF // PIECES), BF16),
            pltpu.VMEM((BLOCK, PAIR, XM), F32),
            pltpu.VMEM((8, YF), F32),
            pltpu.VMEM((8, YF), F32),
            pltpu.VMEM((16, YF), F32),
            pltpu.VMEM((16, YF), F32),
            pltpu.VMEM((2, 8, 2 * M, ROWS), BF16),
            pltpu.VMEM((4, 4, 2 * M, ROWS), BF16),
            pltpu.VMEM((XM, 2 * XM), BF16),
            pltpu.VMEM((XM, 2 * M), BF16),
            pltpu.VMEM((2 * M, 2 * M), BF16),
            pltpu.VMEM((2, ROWS, M), BF16),
            pltpu.VMEM((4, ROWS, M), BF16),
            pltpu.VMEM((12, 2 * M, M), F32),
            pair_of(4, M, M),
            pair_of(4, M, M),
            pair_of(FACETS, 2, BLOCK, M),
            pair_of(FACETS, 2, BLOCK, M),
            pair_of(FACETS, 2, BLOCK, M),
            pair_of(FACETS, 2, BLOCK, M),
            pair_of(4, 64, 2 * M),
            pair_of(2, 64, 2 * M),
            pltpu.VMEM((4, M, ROWS), BF16),
            pltpu.VMEM((4, M, ROWS), BF16),
            dma, dma((PIECES,)), dma,
            dma((4,)), dma((4,)),
            dma((PAIR, 4)), dma((PAIR, 4)),
            dma((PAIR,)), dma((PAIR,)),
            dma((PAIR,)), dma((PAIR,)),
            dma((PAIR, 4)), dma((PAIR, 4)),
            dma((4,)), dma((4,)),
        ],
        compiler_params=pltpu.CompilerParams(
            collective_id=0, has_side_effects=True, vmem_limit_bytes=VMEM_MIB * 2**20
        ),
        cost_estimate=pl.CostEstimate(flops=3 * 10**9, bytes_accessed=4 * 10**6, transcendentals=0),
        name="round_trip",
    )(facets, weights, offsets)
    parts = 4
    update, spectra = pl.pallas_call(
        correction,
        out_shape=(
            jax.ShapeDtypeStruct((1, 2, ROWS, YF), BF16),
            jax.ShapeDtypeStruct((BLOCK, PAIR, 2, XM), F32),
        ),
        in_specs=[vmem, vmem, anywhere],
        out_specs=(hbm, hbm),
        scratch_shapes=[
            pltpu.VMEM((parts, 2, ROWS, YF // parts), BF16),
            dma((parts + 1,)),
        ],
        compiler_params=pltpu.CompilerParams(vmem_limit_bytes=24 * 2**20),
        cost_estimate=pl.CostEstimate(flops=10**9, bytes_accessed=3 * 10**6, transcendentals=0),
        name="correction",
    )(et, q, spectra)
    return update, spectra


def solution(mesh):
    return jax.shard_map(
        shards,
        mesh=mesh,
        in_specs=(
            P("facet", None, ("half", "sub"), None),
            P("facet", ("half", "sub"), None),
            P(),
            P(),
            P(),
        ),
        out_specs=(
            P("facet", None, ("half", "sub"), None),
            P("facet", ("half", "sub"), None, None),
        ),
        check_vma=False,
    )
```

```python
import functools
import math

import jax
import jax.numpy as jnp
from jax import lax
from jax.experimental import pallas as pl
from jax.experimental.pallas import tpu as pltpu
from jax.sharding import PartitionSpec as P

YF = 2048
M = 128
XM = 512
SUBS = 16
FACETS = 32
PAIR = 2
ROWS = 256
BLOCK = 16
PIECES = 4
VMEM_MIB = 52
MESH = pl.DeviceIdType.MESH
F32 = jnp.float32
BF16 = jnp.bfloat16


def cis(turn, n):
    quarter = n // 4
    q = lax.shift_right_logical(turn + n // 8, quarter.bit_length() - 1)
    x = (turn - q * quarter).astype(F32) * (2.0 * math.pi / n)
    z = x * x
    s = x + x * z * (-1.6666654611e-1 + z * (8.3321608736e-3 - 1.9515295891e-4 * z))
    c = 1.0 - 0.5 * z + z * z * (4.166664568298827e-2 + z * (-1.388731625493765e-3 + 2.443315711809948e-5 * z))
    swap = (q & 1) == 1
    cosine = jnp.where(swap, s, c)
    sine = jnp.where(swap, c, s)
    cosine = jnp.where(((q + 1) & 2) != 0, -cosine, cosine)
    sine = jnp.where((q & 2) != 0, -sine, sine)
    return cosine, sine


def iota(shape, dim):
    return lax.broadcasted_iota(jnp.int32, shape, dim)


def taper(pos):
    _, s = cis(2 * pos + 1, 4 * YF)
    return s * s * (1.0 / math.sqrt(YF))


def dot(a, b):
    return jnp.dot(a, b, preferred_element_type=F32)


def dot_t(a, b):
    return lax.dot_general(a, b, (((0,), (0,)), ((), ())), preferred_element_type=F32)


def remote(src, dst, send, recv, to):
    return pltpu.make_async_remote_copy(
        src_ref=src, dst_ref=dst, send_sem=send, recv_sem=recv, device_id=to, device_id_type=MESH
    )


def round_trip(
    facets, weights, offsets_in,
    et_out, q_turned, spectra,
    q_out, offsets, x_buf, w_buf, hi_c, hi_s, lo_c, lo_s, p_tab, p_wide, f_tab, r_tab, perm,
    a_low, a_high, kept, send1, recv1, send2, recv2, send3, recv3, recv4, recv4y, send5, recv5,
    small_sem, x_sem, w_sem, sa, ra, s1, r1, s2, r2, s3, r3, s4, r4, s5, r5,
):
    mine = lax.axis_index("facet")
    x = lax.axis_index("half")
    hi = lax.axis_index("sub")
    core = lax.rem(mine, 2)
    z = lax.rem(mine // 2, 8)
    low = mine // 16

    def at_x(d):
        return {"half": lax.rem(x + d, 4)}

    def peer(i, dy, dc):
        dz = 4 + ((i + 1) // 2) * (1 - 2 * lax.rem(i, 2))
        return lax.rem(low + dy, 2) * 16 + lax.rem(z + dz, 8) * 2 + lax.rem(core + dc, 2)

    across = {"sub": 1 - hi}

    load_o = pltpu.make_async_copy(offsets_in, offsets, small_sem)
    load_o.start()
    width = YF // PIECES
    loads = [
        pltpu.make_async_copy(facets.at[0, :, :, pl.ds(width * i, width)], x_buf.at[i], x_sem.at[i])
        for i in range(PIECES)
    ]
    for load in loads:
        load.start()
    load_w = pltpu.make_async_copy(weights, w_buf, w_sem)
    load_w.start()

    barrier = pltpu.get_barrier_semaphore()
    friends = [across] + [at_x(d) for d in (1, 2, 3)]
    for to in friends:
        pl.semaphore_signal(barrier, inc=1, device_id=to, device_id_type=MESH)

    @pl.loop(1, FACETS)
    def _(i):
        to = {"facet": lax.rem(mine + i, FACETS)}
        pl.semaphore_signal(barrier, inc=1, device_id=to, device_id_type=MESH)

    y = iota((8, YF), 1)
    c, s = cis(iota((16, YF), 0) * iota((16, YF), 1) & (YF - 1), YF)
    w = taper(iota((1, YF), 1))
    lo_c[...] = c * w
    lo_s[...] = s * w
    load_o.wait()
    c, s = cis(((offsets[3, 0] + 16 * iota((8, YF), 0)) & (YF - 1)) * y & (YF - 1), YF)
    hi_c[...] = c
    hi_s[...] = s

    @pl.loop(0, 8)
    def _(a):
        hc, hs = hi_c[pl.ds(a, 1), :], hi_s[pl.ds(a, 1), :]
        lc, ls = lo_c[...], lo_s[...]
        at = pl.multiple_of(a * 16, 16)
        q_out[pl.ds(at, 16), :] = (hc * lc - hs * ls).astype(BF16)
        q_out[pl.ds(at + M, 16), :] = (-(hs * lc + hc * ls)).astype(BF16)

    turn = offsets[1, mine] & (M - 1)
    r, c = iota((2 * M, 2 * M), 0), iota((2 * M, 2 * M), 1)
    k = lax.shift_right_logical(c, 7) * 64 + (c & 63)
    same = ((r & (M - 1)) == ((k - turn) & (M - 1))) & (lax.shift_right_logical(r, 7) == (lax.shift_right_logical(c, 6) & 1))
    perm[...] = jnp.where(same, 1.0, 0.0).astype(BF16)

    over = (((1,), (1,)), ((), ()))
    from_real = from_imag = None
    for i, load in enumerate(loads):
        load.wait()
        q = q_out[:, width * i : width * i + width]
        real = lax.dot_general(x_buf[i, 0], q, over, preferred_element_type=F32)
        imag = lax.dot_general(x_buf[i, 1], q, over, preferred_element_type=F32)
        from_real = real if i == 0 else from_real + real
        from_imag = imag if i == 0 else from_imag + imag
    a_both = jnp.concatenate(
        [from_real[:, :M] - from_imag[:, M:], from_real[:, M:] + from_imag[:, :M]], 1
    ).astype(BF16)
    a_both = dot(a_both, perm[...]).astype(BF16)
    a_low[hi] = a_both[:, :M]
    a_high[x] = a_both[:, M:]

    pl.semaphore_wait(barrier, len(friends) + FACETS - 1)

    def swap_a(d):
        if d:
            return remote(a_high.at[x], a_high.at[x], sa.at[d], ra.at[d], at_x(d))
        return remote(a_low.at[hi], a_low.at[hi], sa.at[0], ra.at[0], across)

    for d in (2, 0, 1, 3):
        swap_a(d).start()

    first = x * (2 * ROWS)
    pos = first + iota((16, 2 * ROWS), 1)
    c, s = cis(iota((16, 2 * ROWS), 0) * pos & (YF - 1), YF)
    w = taper(first + iota((1, 2 * ROWS), 1))
    lc, ls, lc_less, ls_less = c * w, s * w, c * -w, s * -w

    @pl.loop(0, 2 * 4)
    def _(u):
        freq = (offsets[2, 4 * (u // 2) + 2 * hi + lax.rem(u, 2)] + 16 * iota((8, 2 * ROWS), 0)) & (YF - 1)
        hc, hs = cis(freq * (first + iota((8, 2 * ROWS), 1)) & (YF - 1), YF)
        for a in range(8):
            c, s = hc[a : a + 1], hs[a : a + 1]
            real = (c * lc - s * ls).astype(BF16)
            imag = (s * lc_less + c * ls_less).astype(BF16)
            for b in range(2):
                p_tab[b, u, 16 * a : 16 * a + 16, :] = real[:, ROWS * b : ROWS * b + ROWS]
                p_tab[b, u, M + 16 * a : M + 16 * a + 16, :] = imag[:, ROWS * b : ROWS * b + ROWS]

    for b in range(4):
        first_b = (2 * b + hi) * ROWS
        c, s = cis(iota((16, ROWS), 0) * (first_b + iota((16, ROWS), 1)) & (YF - 1), YF)
        w = taper(first_b + iota((1, ROWS), 1))
        lc_b, ls_b, lc_less_b, ls_less_b = c * w, s * w, c * -w, s * -w

        @pl.loop(0, 4)
        def _(u):
            freq = (offsets[2, 4 * x + u] + 16 * iota((8, ROWS), 0)) & (YF - 1)
            hc, hs = cis(freq * (first_b + iota((8, ROWS), 1)) & (YF - 1), YF)
            for a in range(8):
                c, s = hc[a : a + 1], hs[a : a + 1]
                p_wide[b, u, 16 * a : 16 * a + 16, :] = (c * lc_b - s * ls_b).astype(BF16)
                p_wide[b, u, M + 16 * a : M + 16 * a + 16, :] = (s * lc_less_b + c * ls_less_b).astype(BF16)

    left = iota((M, M), 1) < 64

    def complex_sum(v):
        turned = pltpu.roll(v[M:], 64, 1)
        return v[:M] + jnp.where(left, -turned, turned)

    for u in range(8):
        kept[u] = dot(p_tab[hi, u], a_low[hi])
    for u in range(4):
        kept[8 + u] = dot(p_wide[x, u], a_high[x])

    def partial_low(l, to_x):
        u = 2 * to_x + l
        return complex_sum(kept[u] + dot(p_tab[1 - hi, u], a_low[1 - hi]))

    def partial_high(l, to_hi):
        u = 2 * to_hi + l
        v = kept[8 + u]
        for d in (1, 3, 2):
            v = v + dot(p_wide[lax.rem(x + 4 - d, 4), u], a_high[lax.rem(x + 4 - d, 4)])
        return complex_sum(v)

    def sum1(l, d):
        return remote(send1.at[l, d], recv1.at[l, d], s1.at[l, d], r1.at[l, d], at_x(d) if d else across)

    for d in (0, 1, 3, 2):
        if d:
            block = a_high.at[lax.rem(x + 4 - d, 4)]
            remote(block, block, sa.at[d], ra.at[d], at_x(d)).wait_recv()
        else:
            remote(a_low.at[1 - hi], a_low.at[1 - hi], sa.at[0], ra.at[0], across).wait_recv()
            for d_low in (2, 1, 3):
                send1[0, d_low] = partial_low(0, lax.rem(x + d_low, 4)).astype(BF16)
                sum1(0, d_low).start()
    own = []
    for l in range(PAIR):
        send1[l, 0] = partial_high(l, 1 - hi).astype(BF16)
        sum1(l, 0).start()
        if l:
            for d in (2, 1, 3):
                send1[l, d] = partial_low(l, lax.rem(x + d, 4)).astype(BF16)
                sum1(l, d).start()
    for l in range(PAIR):
        own.append((partial_low(l, x), partial_high(l, hi)))

    q_turned[...] = dot_t(perm[...], q_out[...]).astype(BF16)

    scale = 1.0 / math.sqrt(XM)
    place = (offsets[0, mine] + iota((16, M), 1)) & (XM - 1)
    lc, ls = cis(iota((16, M), 0) * place & (XM - 1), XM)
    lc, ls = lc * scale, ls * scale
    place = (offsets[0, mine] + iota((32, M), 1)) & (XM - 1)
    hc, hs = cis(16 * iota((32, M), 0) * place & (XM - 1), XM)
    for a in range(32):
        c, s = hc[a : a + 1], hs[a : a + 1]
        r_tab[16 * a : 16 * a + 16, :M] = (c * lc - s * ls).astype(BF16)
        r_tab[16 * a : 16 * a + 16, M:] = (s * lc + c * ls).astype(BF16)

    c, s = cis(16 * iota((32, XM), 0) * iota((32, XM), 1) & (XM - 1), XM)
    lc, ls = cis(iota((16, XM), 0) * iota((16, XM), 1) & (XM - 1), XM)
    lc, ls = lc * scale, ls * scale
    for a in range(32):
        hc, hs = c[a : a + 1], s[a : a + 1]
        f_tab[16 * a : 16 * a + 16, :XM] = (hc * lc - hs * ls).astype(BF16)
        f_tab[16 * a : 16 * a + 16, XM:] = (hs * lc + hc * ls).astype(BF16)

    def bulk(send, recv, l, ssem, rsem):
        some = pl.ds(0, FACETS - 1)
        return remote(send.at[l, some], recv.at[l, some], ssem.at[l], rsem.at[l], {"facet": peer(0, 0, 0)})

    def to_all(action, first=1):
        for dc in (first, 1 - first):

            @pl.loop(0, 7 + dc)
            def _(i):
                for dy in (1, 0):
                    action(peer(i, dy, dc))

            if dc == 0:
                action(peer(7, 1, 0))

    for l in range(PAIR):
        low_k, high_k = own[l]
        for d in (0, 1, 3, 2):
            sum1(l, d).wait_recv()
            if d:
                low_k = low_k + recv1[l, d].astype(F32)
            else:
                high_k = high_k + recv1[l, d].astype(F32)
        cr = jnp.where(left, low_k, pltpu.roll(high_k, 64, 1)).astype(BF16)
        ci = jnp.where(left, pltpu.roll(low_k, 64, 1), high_k).astype(BF16)
        both = jnp.concatenate([jnp.concatenate([cr, ci], 1), jnp.concatenate([ci, -cr], 1)], 0)
        kk = dot(r_tab[...], both).astype(BF16)
        send2[l, :, 0] = kk[:, :M].reshape(FACETS, BLOCK, M)
        send2[l, :, 1] = kk[:, M:].reshape(FACETS, BLOCK, M)
        to_all(lambda f: remote(send2.at[l, f], recv2.at[l, mine], s2.at[l], r2.at[l], {"facet": f}).start(), 1 - l)
        recv2[l, mine] = send2[l, mine]

    lane = iota((BLOCK, M), 1)

    def tiles_of(f):
        o = offsets[1, f]
        return (lax.shift_right_logical(o, 7) + jnp.where(lane < (o & (M - 1)), 1, 0)) & 3

    load_w.wait()
    for l in range(PAIR):
        bulk(send2, recv2, l, s2, r2).wait_recv()

        def gather(i, acc):
            for f in (2 * i, 2 * i + 1):
                tile = tiles_of(f)
                got = [recv2[l, f, part].astype(F32) for part in range(2)]
                acc = tuple(
                    acc[4 * part + t] + jnp.where(tile == t, got[part], 0.0) for part in range(2) for t in range(4)
                )
            return acc

        acc = lax.fori_loop(0, FACETS // 2, gather, (jnp.zeros((BLOCK, M), F32),) * 8)
        g = jnp.concatenate([jnp.concatenate(acc[:4], 1), jnp.concatenate(acc[4:], 1)], 0).astype(BF16)
        v = dot(g, f_tab[...])
        weight = w_buf[:, l, :]
        h_real = weight * (v[:BLOCK, :XM] + v[BLOCK:, XM:])
        h_imag = weight * (v[BLOCK:, :XM] - v[:BLOCK, XM:])
        v = dot(jnp.concatenate([h_real, h_imag], 0).astype(BF16), f_tab[...])
        space = [v[:BLOCK, :XM] - v[BLOCK:, XM:], v[BLOCK:, :XM] + v[:BLOCK, XM:]]

        def window(f):
            tile = tiles_of(f)
            for part in range(2):
                cut = [space[part][:, M * t : M * t + M] for t in range(4)]
                one = jnp.where(tile == 1, cut[1], cut[0])
                two = jnp.where(tile == 3, cut[3], cut[2])
                send3[l, f, part] = jnp.where(tile < 2, one, two).astype(BF16)

        def window_out(f):
            window(f)
            remote(send3.at[l, f], recv3.at[l, mine], s3.at[l], r3.at[l], {"facet": f}).start()

        to_all(window_out, 1 - l)
        window(mine)
        recv3[l, mine] = send3[l, mine]
        spectra[:, l, 0, :] = h_real
        spectra[:, l, 1, :] = h_imag

    def send4(l, d):
        if d:
            return remote(recv4.at[l, x], recv4.at[l, x], s4.at[l, d], r4.at[l, d], at_x(d))
        return remote(recv4y.at[l, hi], recv4y.at[l, hi], s4.at[l, 0], r4.at[l, 0], across)

    def swap_e(d):
        return remote(send5.at[d], recv5.at[d], s5.at[d], r5.at[d], at_x(d) if d else across)

    for l in range(PAIR):
        bulk(send3, recv3, l, s3, r3).wait_recv()
        rows = jnp.concatenate([recv3[l, :, 0].reshape(XM, M), recv3[l, :, 1].reshape(XM, M)], 1)
        u = dot_t(rows, r_tab[...])
        d_both = jnp.concatenate([u[:M, :M] - u[M:, M:], u[M:, :M] + u[:M, M:]], 1).astype(BF16)
        recv4[l, x] = d_both[:64]
        recv4y[l, hi] = d_both[64:]
        for d in (2, 0, 1, 3):
            send4(l, d).start()

    def twice(v):
        return jnp.concatenate([v, jnp.concatenate([v[:, M:], -v[:, :M]], 1)], 0)

    def add(total, term):
        return term if total is None else total + term

    low_e, high_e = [None, None], [None] * 4
    for l in range(PAIR):
        for d in (0, 1, 3, 2):
            from_x = lax.rem(x + 4 - d, 4)
            if d:
                block = recv4.at[l, from_x]
                remote(block, block, s4.at[l, d], r4.at[l, d], at_x(d)).wait_recv()
            else:
                block = recv4y.at[l, 1 - hi]
                remote(block, block, s4.at[l, d], r4.at[l, d], across).wait_recv()
                for near_hi in (hi, 1 - hi):
                    v = twice(recv4y[l, near_hi])
                    for e in (2, 1, 3) if l else (2, 1, 3, 0):
                        high_e[e] = add(high_e[e], dot(v, p_wide[lax.rem(x + e, 4), 2 * near_hi + l]))
                if l:
                    for e in (2, 1, 3):
                        send5[e] = high_e[e].astype(BF16)
                        swap_e(e).start()
            v = twice(recv4[l, from_x])
            low_e[1] = add(low_e[1], dot(v, p_tab[1 - hi, 2 * from_x + l]))
            if l == 0:
                low_e[0] = add(low_e[0], dot(v, p_tab[hi, 2 * from_x]))
    send5[0] = low_e[1].astype(BF16)
    swap_e(0).start()
    for d in range(4):
        from_x = lax.rem(x + 4 - d, 4)
        low_e[0] = low_e[0] + dot(twice(recv4[1, from_x]), p_tab[hi, 2 * from_x + 1])
    for near_hi in range(2):
        high_e[0] = high_e[0] + dot(twice(recv4y[1, near_hi]), p_wide[x, 2 * near_hi + 1])
    for l in range(PAIR):
        bulk(send2, recv2, l, s2, r2).wait_send()
        bulk(send3, recv3, l, s3, r3).wait_send()
        for d in range(4):
            sum1(l, d).wait_send()
            send4(l, d).wait_send()
    for d in range(4):
        swap_a(d).wait_send()
    low_k, high_k = low_e[0], high_e[0]
    for d in (1, 3, 2, 0):
        swap_e(d).wait_recv()
        if d:
            high_k = high_k + recv5[d].astype(F32)
        else:
            low_k = low_k + recv5[d].astype(F32)
    et_out[...] = jnp.concatenate([low_k, high_k], 0).astype(BF16)
    for d in range(4):
        swap_e(d).wait_send()


def correction(et, q, spectra_in, out, spectra_out, buf, sems):
    parts = buf.shape[0]
    width = buf.shape[3]
    moves = [pltpu.make_async_copy(spectra_in, spectra_out, sems.at[parts])]
    moves[0].start()
    gain = 2.0 * math.sqrt(YF / M)
    real = et[...]
    imag = jnp.concatenate([real[64:128], -real[:64], real[192:], -real[128:192]], 0)
    for i in range(parts):
        table = q[:, width * i : width * i + width]
        buf[i, 0] = (dot_t(real, table) * gain).astype(BF16)
        buf[i, 1] = (dot_t(imag, table) * gain).astype(BF16)
        moves.append(pltpu.make_async_copy(buf.at[i], out.at[0, :, :, pl.ds(width * i, width)], sems.at[i]))
        moves[-1].start()
    for move in moves:
        move.wait()


def shards(facets, weights, facet_offsets, subgrid_offsets, column):
    hbm = pl.BlockSpec(memory_space=pltpu.HBM)
    anywhere = pl.BlockSpec(memory_space=pl.ANY)
    vmem = pl.BlockSpec(memory_space=pltpu.VMEM)
    dma = pltpu.SemaphoreType.DMA
    pair_of = lambda *shape: pltpu.VMEM((PAIR, *shape), BF16)
    zero = jnp.int32(0)
    offsets = (
        lax.pad(facet_offsets.T, zero, [(0, 2, 0), (0, 0, 0)])
        + lax.pad(subgrid_offsets[None], zero, [(2, 1, 0), (0, FACETS - SUBS, 0)])
        + lax.pad(column[None], zero, [(3, 0, 0), (0, FACETS - 1, 0)])
    )
    et, q, spectra = pl.pallas_call(
        round_trip,
        out_shape=(
            jax.ShapeDtypeStruct((2 * M, ROWS), BF16),
            jax.ShapeDtypeStruct((2 * M, YF), BF16),
            jax.ShapeDtypeStruct((BLOCK, PAIR, 2, XM), F32),
        ),
        in_specs=[hbm] * 3,
        out_specs=(vmem, vmem, vmem),
        scratch_shapes=[
            pltpu.VMEM((2 * M, YF), BF16),
            pltpu.SMEM((4, FACETS), jnp.int32),
            pltpu.VMEM((PIECES, 2, ROWS, YF // PIECES), BF16),
            pltpu.VMEM((BLOCK, PAIR, XM), F32),
            pltpu.VMEM((8, YF), F32),
            pltpu.VMEM((8, YF), F32),
            pltpu.VMEM((16, YF), F32),
            pltpu.VMEM((16, YF), F32),
            pltpu.VMEM((2, 8, 2 * M, ROWS), BF16),
            pltpu.VMEM((4, 4, 2 * M, ROWS), BF16),
            pltpu.VMEM((XM, 2 * XM), BF16),
            pltpu.VMEM((XM, 2 * M), BF16),
            pltpu.VMEM((2 * M, 2 * M), BF16),
            pltpu.VMEM((2, ROWS, M), BF16),
            pltpu.VMEM((4, ROWS, M), BF16),
            pltpu.VMEM((12, 2 * M, M), F32),
            pair_of(4, M, M),
            pair_of(4, M, M),
            pair_of(FACETS, 2, BLOCK, M),
            pair_of(FACETS, 2, BLOCK, M),
            pair_of(FACETS, 2, BLOCK, M),
            pair_of(FACETS, 2, BLOCK, M),
            pair_of(4, 64, 2 * M),
            pair_of(2, 64, 2 * M),
            pltpu.VMEM((4, M, ROWS), BF16),
            pltpu.VMEM((4, M, ROWS), BF16),
            dma, dma((PIECES,)), dma,
            dma((4,)), dma((4,)),
            dma((PAIR, 4)), dma((PAIR, 4)),
            dma((PAIR,)), dma((PAIR,)),
            dma((PAIR,)), dma((PAIR,)),
            dma((PAIR, 4)), dma((PAIR, 4)),
            dma((4,)), dma((4,)),
        ],
        compiler_params=pltpu.CompilerParams(
            collective_id=0, has_side_effects=True, vmem_limit_bytes=VMEM_MIB * 2**20
        ),
        cost_estimate=pl.CostEstimate(flops=3 * 10**9, bytes_accessed=4 * 10**6, transcendentals=0),
        name="round_trip",
    )(facets, weights, offsets)
    parts = 4
    update, spectra = pl.pallas_call(
        correction,
        out_shape=(
            jax.ShapeDtypeStruct((1, 2, ROWS, YF), BF16),
            jax.ShapeDtypeStruct((BLOCK, PAIR, 2, XM), F32),
        ),
        in_specs=[vmem, vmem, anywhere],
        out_specs=(hbm, hbm),
        scratch_shapes=[
            pltpu.VMEM((parts, 2, ROWS, YF // parts), BF16),
            dma((parts + 1,)),
        ],
        compiler_params=pltpu.CompilerParams(vmem_limit_bytes=24 * 2**20),
        cost_estimate=pl.CostEstimate(flops=10**9, bytes_accessed=3 * 10**6, transcendentals=0),
        name="correction",
    )(et, q, spectra)
    return update, spectra


def solution(mesh):
    return jax.shard_map(
        shards,
        mesh=mesh,
        in_specs=(
            P("facet", None, ("half", "sub"), None),
            P("facet", ("half", "sub"), None),
            P(),
            P(),
            P(),
        ),
        out_specs=(
            P("facet", None, ("half", "sub"), None),
            P("facet", ("half", "sub"), None, None),
        ),
        check_vma=False,
    )
```

```python
import functools
import math

import jax
import jax.numpy as jnp
from jax import lax
from jax.experimental import pallas as pl
from jax.experimental.pallas import tpu as pltpu
from jax.sharding import PartitionSpec as P

YF = 2048
M = 128
XM = 512
SUBS = 16
FACETS = 32
PAIR = 2
ROWS = 256
BLOCK = 16
PIECES = 4
VMEM_MIB = 52
MESH = pl.DeviceIdType.MESH
F32 = jnp.float32
BF16 = jnp.bfloat16


def cis(turn, n):
    quarter = n // 4
    q = lax.shift_right_logical(turn + n // 8, quarter.bit_length() - 1)
    x = (turn - q * quarter).astype(F32) * (2.0 * math.pi / n)
    z = x * x
    s = x + x * z * (-1.6666654611e-1 + z * (8.3321608736e-3 - 1.9515295891e-4 * z))
    c = 1.0 - 0.5 * z + z * z * (4.166664568298827e-2 + z * (-1.388731625493765e-3 + 2.443315711809948e-5 * z))
    swap = (q & 1) == 1
    cosine = jnp.where(swap, s, c)
    sine = jnp.where(swap, c, s)
    cosine = jnp.where(((q + 1) & 2) != 0, -cosine, cosine)
    sine = jnp.where((q & 2) != 0, -sine, sine)
    return cosine, sine


def iota(shape, dim):
    return lax.broadcasted_iota(jnp.int32, shape, dim)


def taper(pos):
    _, s = cis(2 * pos + 1, 4 * YF)
    return s * s * (1.0 / math.sqrt(YF))


def dot(a, b):
    return jnp.dot(a, b, preferred_element_type=F32)


def dot_t(a, b):
    return lax.dot_general(a, b, (((0,), (0,)), ((), ())), preferred_element_type=F32)


def remote(src, dst, send, recv, to):
    return pltpu.make_async_remote_copy(
        src_ref=src, dst_ref=dst, send_sem=send, recv_sem=recv, device_id=to, device_id_type=MESH
    )


def round_trip(
    facets, weights, offsets_in,
    et_out, q_turned, spectra,
    q_out, offsets, x_buf, w_buf, hi_c, hi_s, lo_c, lo_s, p_tab, p_wide, f_tab, r_tab, perm,
    a_low, a_high, kept, send1, recv1, send2, recv2, send3, recv3, recv4, recv4y, send5, recv5,
    small_sem, x_sem, w_sem, sa, ra, s1, r1, s2, r2, s3, r3, s4, r4, s5, r5,
):
    mine = lax.axis_index("facet")
    x = lax.axis_index("half")
    hi = lax.axis_index("sub")
    core = lax.rem(mine, 2)
    z = lax.rem(mine // 2, 8)
    low = mine // 16

    def at_x(d):
        return {"half": lax.rem(x + d, 4)}

    def peer(i, dy, dc):
        dz = 4 + ((i + 1) // 2) * (1 - 2 * lax.rem(i, 2))
        return lax.rem(low + dy, 2) * 16 + lax.rem(z + dz, 8) * 2 + lax.rem(core + dc, 2)

    across = {"sub": 1 - hi}

    load_o = pltpu.make_async_copy(offsets_in, offsets, small_sem)
    load_o.start()
    width = YF // PIECES
    loads = [
        pltpu.make_async_copy(facets.at[0, :, :, pl.ds(width * i, width)], x_buf.at[i], x_sem.at[i])
        for i in range(PIECES)
    ]
    for load in loads:
        load.start()
    load_w = pltpu.make_async_copy(weights, w_buf, w_sem)
    load_w.start()

    barrier = pltpu.get_barrier_semaphore()
    friends = [across] + [at_x(d) for d in (1, 2, 3)]
    for to in friends:
        pl.semaphore_signal(barrier, inc=1, device_id=to, device_id_type=MESH)

    @pl.loop(1, FACETS)
    def _(i):
        to = {"facet": lax.rem(mine + i, FACETS)}
        pl.semaphore_signal(barrier, inc=1, device_id=to, device_id_type=MESH)

    y = iota((8, YF), 1)
    c, s = cis(iota((16, YF), 0) * iota((16, YF), 1) & (YF - 1), YF)
    w = taper(iota((1, YF), 1))
    lo_c[...] = c * w
    lo_s[...] = s * w
    load_o.wait()
    c, s = cis(((offsets[3, 0] + 16 * iota((8, YF), 0)) & (YF - 1)) * y & (YF - 1), YF)
    hi_c[...] = c
    hi_s[...] = s

    @pl.loop(0, 8)
    def _(a):
        hc, hs = hi_c[pl.ds(a, 1), :], hi_s[pl.ds(a, 1), :]
        lc, ls = lo_c[...], lo_s[...]
        at = pl.multiple_of(a * 16, 16)
        q_out[pl.ds(at, 16), :] = (hc * lc - hs * ls).astype(BF16)
        q_out[pl.ds(at + M, 16), :] = (-(hs * lc + hc * ls)).astype(BF16)

    turn = offsets[1, mine] & (M - 1)
    r, c = iota((2 * M, 2 * M), 0), iota((2 * M, 2 * M), 1)
    k = lax.shift_right_logical(c, 7) * 64 + (c & 63)
    same = ((r & (M - 1)) == ((k - turn) & (M - 1))) & (lax.shift_right_logical(r, 7) == (lax.shift_right_logical(c, 6) & 1))
    perm[...] = jnp.where(same, 1.0, 0.0).astype(BF16)

    over = (((1,), (1,)), ((), ()))
    from_real = from_imag = None
    for i, load in enumerate(loads):
        load.wait()
        q = q_out[:, width * i : width * i + width]
        real = lax.dot_general(x_buf[i, 0], q, over, preferred_element_type=F32)
        imag = lax.dot_general(x_buf[i, 1], q, over, preferred_element_type=F32)
        from_real = real if i == 0 else from_real + real
        from_imag = imag if i == 0 else from_imag + imag
    a_both = jnp.concatenate(
        [from_real[:, :M] - from_imag[:, M:], from_real[:, M:] + from_imag[:, :M]], 1
    ).astype(BF16)
    a_both = dot(a_both, perm[...]).astype(BF16)
    a_low[hi] = a_both[:, :M]
    a_high[x] = a_both[:, M:]

    pl.semaphore_wait(barrier, len(friends) + FACETS - 1)

    def swap_a(d):
        if d:
            return remote(a_high.at[x], a_high.at[x], sa.at[d], ra.at[d], at_x(d))
        return remote(a_low.at[hi], a_low.at[hi], sa.at[0], ra.at[0], across)

    for d in (2, 0, 1, 3):
        swap_a(d).start()

    first = x * (2 * ROWS)
    pos = first + iota((16, 2 * ROWS), 1)
    c, s = cis(iota((16, 2 * ROWS), 0) * pos & (YF - 1), YF)
    w = taper(first + iota((1, 2 * ROWS), 1))
    lc, ls, lc_less, ls_less = c * w, s * w, c * -w, s * -w

    @pl.loop(0, 2 * 4)
    def _(u):
        freq = (offsets[2, 4 * (u // 2) + 2 * hi + lax.rem(u, 2)] + 16 * iota((8, 2 * ROWS), 0)) & (YF - 1)
        hc, hs = cis(freq * (first + iota((8, 2 * ROWS), 1)) & (YF - 1), YF)
        for a in range(8):
            c, s = hc[a : a + 1], hs[a : a + 1]
            real = (c * lc - s * ls).astype(BF16)
            imag = (s * lc_less + c * ls_less).astype(BF16)
            for b in range(2):
                p_tab[b, u, 16 * a : 16 * a + 16, :] = real[:, ROWS * b : ROWS * b + ROWS]
                p_tab[b, u, M + 16 * a : M + 16 * a + 16, :] = imag[:, ROWS * b : ROWS * b + ROWS]

    for b in range(4):
        first_b = (2 * b + hi) * ROWS
        c, s = cis(iota((16, ROWS), 0) * (first_b + iota((16, ROWS), 1)) & (YF - 1), YF)
        w = taper(first_b + iota((1, ROWS), 1))
        lc_b, ls_b, lc_less_b, ls_less_b = c * w, s * w, c * -w, s * -w

        @pl.loop(0, 4)
        def _(u):
            freq = (offsets[2, 4 * x + u] + 16 * iota((8, ROWS), 0)) & (YF - 1)
            hc, hs = cis(freq * (first_b + iota((8, ROWS), 1)) & (YF - 1), YF)
            for a in range(8):
                c, s = hc[a : a + 1], hs[a : a + 1]
                p_wide[b, u, 16 * a : 16 * a + 16, :] = (c * lc_b - s * ls_b).astype(BF16)
                p_wide[b, u, M + 16 * a : M + 16 * a + 16, :] = (s * lc_less_b + c * ls_less_b).astype(BF16)

    left = iota((M, M), 1) < 64

    def complex_sum(v):
        turned = pltpu.roll(v[M:], 64, 1)
        return v[:M] + jnp.where(left, -turned, turned)

    for u in range(8):
        kept[u] = dot(p_tab[hi, u], a_low[hi])
    for u in range(4):
        kept[8 + u] = dot(p_wide[x, u], a_high[x])

    def partial_low(l, to_x):
        u = 2 * to_x + l
        return complex_sum(kept[u] + dot(p_tab[1 - hi, u], a_low[1 - hi]))

    def partial_high(l, to_hi):
        u = 2 * to_hi + l
        v = kept[8 + u]
        for d in (1, 3, 2):
            v = v + dot(p_wide[lax.rem(x + 4 - d, 4), u], a_high[lax.rem(x + 4 - d, 4)])
        return complex_sum(v)

    def sum1(l, d):
        return remote(send1.at[l, d], recv1.at[l, d], s1.at[l, d], r1.at[l, d], at_x(d) if d else across)

    for d in (0, 1, 3, 2):
        if d:
            block = a_high.at[lax.rem(x + 4 - d, 4)]
            remote(block, block, sa.at[d], ra.at[d], at_x(d)).wait_recv()
        else:
            remote(a_low.at[1 - hi], a_low.at[1 - hi], sa.at[0], ra.at[0], across).wait_recv()
            for d_low in (2, 1, 3):
                send1[0, d_low] = partial_low(0, lax.rem(x + d_low, 4)).astype(BF16)
                sum1(0, d_low).start()
    own = []
    for l in range(PAIR):
        send1[l, 0] = partial_high(l, 1 - hi).astype(BF16)
        sum1(l, 0).start()
        if l:
            for d in (2, 1, 3):
                send1[l, d] = partial_low(l, lax.rem(x + d, 4)).astype(BF16)
                sum1(l, d).start()
    for l in range(PAIR):
        own.append((partial_low(l, x), partial_high(l, hi)))

    q_turned[...] = dot_t(perm[...], q_out[...]).astype(BF16)

    scale = 1.0 / math.sqrt(XM)
    place = (offsets[0, mine] + iota((16, M), 1)) & (XM - 1)
    lc, ls = cis(iota((16, M), 0) * place & (XM - 1), XM)
    lc, ls = lc * scale, ls * scale
    place = (offsets[0, mine] + iota((32, M), 1)) & (XM - 1)
    hc, hs = cis(16 * iota((32, M), 0) * place & (XM - 1), XM)
    for a in range(32):
        c, s = hc[a : a + 1], hs[a : a + 1]
        r_tab[16 * a : 16 * a + 16, :M] = (c * lc - s * ls).astype(BF16)
        r_tab[16 * a : 16 * a + 16, M:] = (s * lc + c * ls).astype(BF16)

    c, s = cis(16 * iota((32, XM), 0) * iota((32, XM), 1) & (XM - 1), XM)
    lc, ls = cis(iota((16, XM), 0) * iota((16, XM), 1) & (XM - 1), XM)
    lc, ls = lc * scale, ls * scale
    for a in range(32):
        hc, hs = c[a : a + 1], s[a : a + 1]
        f_tab[16 * a : 16 * a + 16, :XM] = (hc * lc - hs * ls).astype(BF16)
        f_tab[16 * a : 16 * a + 16, XM:] = (hs * lc + hc * ls).astype(BF16)

    def bulk(send, recv, l, ssem, rsem):
        some = pl.ds(0, FACETS - 1)
        return remote(send.at[l, some], recv.at[l, some], ssem.at[l], rsem.at[l], {"facet": peer(0, 0, 0)})

    def to_all(action, first=1):
        for dc in (first, 1 - first):
            for i in range(8):
                for dy in (1, 0):
                    if dc or dy or i < 7:
                        action(peer(jnp.int32(i), dy, dc))

    for l in range(PAIR):
        low_k, high_k = own[l]
        for d in (0, 1, 3, 2):
            sum1(l, d).wait_recv()
            if d:
                low_k = low_k + recv1[l, d].astype(F32)
            else:
                high_k = high_k + recv1[l, d].astype(F32)
        cr = jnp.where(left, low_k, pltpu.roll(high_k, 64, 1)).astype(BF16)
        ci = jnp.where(left, pltpu.roll(low_k, 64, 1), high_k).astype(BF16)
        both = jnp.concatenate([jnp.concatenate([cr, ci], 1), jnp.concatenate([ci, -cr], 1)], 0)
        kk = dot(r_tab[...], both).astype(BF16)
        send2[l, :, 0] = kk[:, :M].reshape(FACETS, BLOCK, M)
        send2[l, :, 1] = kk[:, M:].reshape(FACETS, BLOCK, M)
        to_all(lambda f: remote(send2.at[l, f], recv2.at[l, mine], s2.at[l], r2.at[l], {"facet": f}).start(), 1 - l)
        recv2[l, mine] = send2[l, mine]

    lane = iota((BLOCK, M), 1)

    def tiles_of(f):
        o = offsets[1, f]
        return (lax.shift_right_logical(o, 7) + jnp.where(lane < (o & (M - 1)), 1, 0)) & 3

    load_w.wait()
    for l in range(PAIR):
        bulk(send2, recv2, l, s2, r2).wait_recv()

        def gather(i, acc):
            for f in (2 * i, 2 * i + 1):
                tile = tiles_of(f)
                got = [recv2[l, f, part].astype(F32) for part in range(2)]
                acc = tuple(
                    acc[4 * part + t] + jnp.where(tile == t, got[part], 0.0) for part in range(2) for t in range(4)
                )
            return acc

        acc = lax.fori_loop(0, FACETS // 2, gather, (jnp.zeros((BLOCK, M), F32),) * 8)
        g = jnp.concatenate([jnp.concatenate(acc[:4], 1), jnp.concatenate(acc[4:], 1)], 0).astype(BF16)
        v = dot(g, f_tab[...])
        weight = w_buf[:, l, :]
        h_real = weight * (v[:BLOCK, :XM] + v[BLOCK:, XM:])
        h_imag = weight * (v[BLOCK:, :XM] - v[:BLOCK, XM:])
        v = dot(jnp.concatenate([h_real, h_imag], 0).astype(BF16), f_tab[...])
        space = [v[:BLOCK, :XM] - v[BLOCK:, XM:], v[BLOCK:, :XM] + v[:BLOCK, XM:]]

        def window(f):
            tile = tiles_of(f)
            for part in range(2):
                cut = [space[part][:, M * t : M * t + M] for t in range(4)]
                one = jnp.where(tile == 1, cut[1], cut[0])
                two = jnp.where(tile == 3, cut[3], cut[2])
                send3[l, f, part] = jnp.where(tile < 2, one, two).astype(BF16)

        def window_out(f):
            window(f)
            remote(send3.at[l, f], recv3.at[l, mine], s3.at[l], r3.at[l], {"facet": f}).start()

        to_all(window_out, 1 - l)
        window(mine)
        recv3[l, mine] = send3[l, mine]
        spectra[:, l, 0, :] = h_real
        spectra[:, l, 1, :] = h_imag

    def send4(l, d):
        if d:
            return remote(recv4.at[l, x], recv4.at[l, x], s4.at[l, d], r4.at[l, d], at_x(d))
        return remote(recv4y.at[l, hi], recv4y.at[l, hi], s4.at[l, 0], r4.at[l, 0], across)

    def swap_e(d):
        return remote(send5.at[d], recv5.at[d], s5.at[d], r5.at[d], at_x(d) if d else across)

    for l in range(PAIR):
        bulk(send3, recv3, l, s3, r3).wait_recv()
        rows = jnp.concatenate([recv3[l, :, 0].reshape(XM, M), recv3[l, :, 1].reshape(XM, M)], 1)
        u = dot_t(rows, r_tab[...])
        d_both = jnp.concatenate([u[:M, :M] - u[M:, M:], u[M:, :M] + u[:M, M:]], 1).astype(BF16)
        recv4[l, x] = d_both[:64]
        recv4y[l, hi] = d_both[64:]
        for d in (2, 0, 1, 3):
            send4(l, d).start()

    def twice(v):
        return jnp.concatenate([v, jnp.concatenate([v[:, M:], -v[:, :M]], 1)], 0)

    def add(total, term):
        return term if total is None else total + term

    low_e, high_e = [None, None], [None] * 4
    for l in range(PAIR):
        for d in (0, 1, 3, 2):
            from_x = lax.rem(x + 4 - d, 4)
            if d:
                block = recv4.at[l, from_x]
                remote(block, block, s4.at[l, d], r4.at[l, d], at_x(d)).wait_recv()
            else:
                block = recv4y.at[l, 1 - hi]
                remote(block, block, s4.at[l, d], r4.at[l, d], across).wait_recv()
                for near_hi in (hi, 1 - hi):
                    v = twice(recv4y[l, near_hi])
                    for e in (2, 1, 3) if l else (2, 1, 3, 0):
                        high_e[e] = add(high_e[e], dot(v, p_wide[lax.rem(x + e, 4), 2 * near_hi + l]))
                if l:
                    for e in (2, 1, 3):
                        send5[e] = high_e[e].astype(BF16)
                        swap_e(e).start()
            v = twice(recv4[l, from_x])
            low_e[1] = add(low_e[1], dot(v, p_tab[1 - hi, 2 * from_x + l]))
            if l == 0:
                low_e[0] = add(low_e[0], dot(v, p_tab[hi, 2 * from_x]))
    send5[0] = low_e[1].astype(BF16)
    swap_e(0).start()
    for d in range(4):
        from_x = lax.rem(x + 4 - d, 4)
        low_e[0] = low_e[0] + dot(twice(recv4[1, from_x]), p_tab[hi, 2 * from_x + 1])
    for near_hi in range(2):
        high_e[0] = high_e[0] + dot(twice(recv4y[1, near_hi]), p_wide[x, 2 * near_hi + 1])
    for l in range(PAIR):
        bulk(send2, recv2, l, s2, r2).wait_send()
        bulk(send3, recv3, l, s3, r3).wait_send()
        for d in range(4):
            sum1(l, d).wait_send()
            send4(l, d).wait_send()
    for d in range(4):
        swap_a(d).wait_send()
    low_k, high_k = low_e[0], high_e[0]
    for d in (1, 3, 2, 0):
        swap_e(d).wait_recv()
        if d:
            high_k = high_k + recv5[d].astype(F32)
        else:
            low_k = low_k + recv5[d].astype(F32)
    et_out[...] = jnp.concatenate([low_k, high_k], 0).astype(BF16)
    for d in range(4):
        swap_e(d).wait_send()


def correction(et, q, spectra_in, out, spectra_out, buf, sems):
    parts = buf.shape[0]
    width = buf.shape[3]
    moves = [pltpu.make_async_copy(spectra_in, spectra_out, sems.at[parts])]
    moves[0].start()
    gain = 2.0 * math.sqrt(YF / M)
    real = et[...]
    imag = jnp.concatenate([real[64:128], -real[:64], real[192:], -real[128:192]], 0)
    for i in range(parts):
        table = q[:, width * i : width * i + width]
        buf[i, 0] = (dot_t(real, table) * gain).astype(BF16)
        buf[i, 1] = (dot_t(imag, table) * gain).astype(BF16)
        moves.append(pltpu.make_async_copy(buf.at[i], out.at[0, :, :, pl.ds(width * i, width)], sems.at[i]))
        moves[-1].start()
    for move in moves:
        move.wait()


def shards(facets, weights, facet_offsets, subgrid_offsets, column):
    hbm = pl.BlockSpec(memory_space=pltpu.HBM)
    anywhere = pl.BlockSpec(memory_space=pl.ANY)
    vmem = pl.BlockSpec(memory_space=pltpu.VMEM)
    dma = pltpu.SemaphoreType.DMA
    pair_of = lambda *shape: pltpu.VMEM((PAIR, *shape), BF16)
    zero = jnp.int32(0)
    offsets = (
        lax.pad(facet_offsets.T, zero, [(0, 2, 0), (0, 0, 0)])
        + lax.pad(subgrid_offsets[None], zero, [(2, 1, 0), (0, FACETS - SUBS, 0)])
        + lax.pad(column[None], zero, [(3, 0, 0), (0, FACETS - 1, 0)])
    )
    et, q, spectra = pl.pallas_call(
        round_trip,
        out_shape=(
            jax.ShapeDtypeStruct((2 * M, ROWS), BF16),
            jax.ShapeDtypeStruct((2 * M, YF), BF16),
            jax.ShapeDtypeStruct((BLOCK, PAIR, 2, XM), F32),
        ),
        in_specs=[hbm] * 3,
        out_specs=(vmem, vmem, vmem),
        scratch_shapes=[
            pltpu.VMEM((2 * M, YF), BF16),
            pltpu.SMEM((4, FACETS), jnp.int32),
            pltpu.VMEM((PIECES, 2, ROWS, YF // PIECES), BF16),
            pltpu.VMEM((BLOCK, PAIR, XM), F32),
            pltpu.VMEM((8, YF), F32),
            pltpu.VMEM((8, YF), F32),
            pltpu.VMEM((16, YF), F32),
            pltpu.VMEM((16, YF), F32),
            pltpu.VMEM((2, 8, 2 * M, ROWS), BF16),
            pltpu.VMEM((4, 4, 2 * M, ROWS), BF16),
            pltpu.VMEM((XM, 2 * XM), BF16),
            pltpu.VMEM((XM, 2 * M), BF16),
            pltpu.VMEM((2 * M, 2 * M), BF16),
            pltpu.VMEM((2, ROWS, M), BF16),
            pltpu.VMEM((4, ROWS, M), BF16),
            pltpu.VMEM((12, 2 * M, M), F32),
            pair_of(4, M, M),
            pair_of(4, M, M),
            pair_of(FACETS, 2, BLOCK, M),
            pair_of(FACETS, 2, BLOCK, M),
            pair_of(FACETS, 2, BLOCK, M),
            pair_of(FACETS, 2, BLOCK, M),
            pair_of(4, 64, 2 * M),
            pair_of(2, 64, 2 * M),
            pltpu.VMEM((4, M, ROWS), BF16),
            pltpu.VMEM((4, M, ROWS), BF16),
            dma, dma((PIECES,)), dma,
            dma((4,)), dma((4,)),
            dma((PAIR, 4)), dma((PAIR, 4)),
            dma((PAIR,)), dma((PAIR,)),
            dma((PAIR,)), dma((PAIR,)),
            dma((PAIR, 4)), dma((PAIR, 4)),
            dma((4,)), dma((4,)),
        ],
        compiler_params=pltpu.CompilerParams(
            collective_id=0, has_side_effects=True, vmem_limit_bytes=VMEM_MIB * 2**20
        ),
        cost_estimate=pl.CostEstimate(flops=3 * 10**9, bytes_accessed=4 * 10**6, transcendentals=0),
        name="round_trip",
    )(facets, weights, offsets)
    parts = 4
    update, spectra = pl.pallas_call(
        correction,
        out_shape=(
            jax.ShapeDtypeStruct((1, 2, ROWS, YF), BF16),
            jax.ShapeDtypeStruct((BLOCK, PAIR, 2, XM), F32),
        ),
        in_specs=[vmem, vmem, anywhere],
        out_specs=(hbm, hbm),
        scratch_shapes=[
            pltpu.VMEM((parts, 2, ROWS, YF // parts), BF16),
            dma((parts + 1,)),
        ],
        compiler_params=pltpu.CompilerParams(vmem_limit_bytes=24 * 2**20),
        cost_estimate=pl.CostEstimate(flops=10**9, bytes_accessed=3 * 10**6, transcendentals=0),
        name="correction",
    )(et, q, spectra)
    return update, spectra


def solution(mesh):
    return jax.shard_map(
        shards,
        mesh=mesh,
        in_specs=(
            P("facet", None, ("half", "sub"), None),
            P("facet", ("half", "sub"), None),
            P(),
            P(),
            P(),
        ),
        out_specs=(
            P("facet", None, ("half", "sub"), None),
            P("facet", ("half", "sub"), None, None),
        ),
        check_vma=False,
    )
```
